512 devices in a mesh: lat: 8 (over y_lo, x), lon: 64 (over y_hi, z, core).
Axes of the slice: x: 4, y: 4 (y_hi: 2, y_lo: 2; y = y_hi * 2 + y_lo), z: 16, core: 2. Of those that a mesh axis runs over, the one named last changes fastest.
Arguments:
- field: bfloat16 [4, 48, 294912], P(None, 'lat', 'lon')
- shift: int32 [2], replicated, may hold values from 1 to 11, as said below
- window_type: int32 [2, 8], replicated, may hold values from 0 to 15
- qkv_weight: bfloat16 [2, 192, 576], replicated
- proj_weight: bfloat16 [2, 192, 192], replicated, may hold values from -0.4375 to 0.4375
- up_weight: bfloat16 [2, 192, 768], replicated, may hold values from -0.4375 to 0.4375
- down_weight: bfloat16 [2, 768, 192], replicated, may hold values from -0.21875 to 0.21875
- bias_table: bfloat16 [2, 16, 6, 3312], replicated, may hold values from -4 to 4
Outputs:
- result: bfloat16 [4, 48, 294912], P(None, 'lat', 'lon')
The draws below stay inside these ranges and needn't reach their ends.
Inputs may be any that keep to these rules, and one draw needn't show every extreme that they name: shift[0] lies in 1 to 5 and shift[1] equals 11.
All inputs are finite; a program needn't handle non-finite values.
Results may differ from the reference program's by a relative error of at most 0.014.
Values may be sent and summed in bfloat16 or wider, within the bound.
No kernel may reach another device: no remote copies, remote signals or barrier semaphores. Data moves between devices by JAX's collectives and lax.ppermute only.
A program may use at most 128 MiB of HBM per device.

```python
import jax
import jax.numpy as jnp
import numpy as np
from jax import lax

C = 192
HEADS = 6
HEAD_DIM = 32
FF_DIM = 768
WPL = 2
WLAT = 6
WLON = 12
PL = 4
TYPES = 16
BIAS_LEN = 3312
NLAT = 48
NLON = 1536
NLATW = 8


def draw_field(key, part):
    key = jax.random.fold_in(key, 11)
    key_base = jax.random.fold_in(key, 0)
    key_scale = jax.random.fold_in(key, 1)
    key_chan = jax.random.fold_in(key, 3)
    base = jax.random.normal(key_base, (PL, NLAT, NLON, C), jnp.float32)
    scale = jnp.exp(jax.random.uniform(key_scale, (PL, NLAT, NLON, 1), jnp.float32, -1.2, 1.2))
    chan_scale = jnp.exp(jax.random.uniform(key_chan, (1, 1, 1, C), jnp.float32, -0.7, 0.7))
    values = base * scale * chan_scale
    return values.reshape(PL, NLAT, NLON * C).astype(jnp.bfloat16)


def draw_shift(key, part):
    key = jax.random.fold_in(key, 12)
    lat_part = jax.random.randint(key, (1,), 1, WLAT, jnp.int32)
    lon_part = jnp.full((1,), WLON - 1, jnp.int32)
    return jnp.concatenate([lat_part, lon_part]).astype(jnp.int32)


def draw_qkv_weight(key, part):
    key = jax.random.fold_in(key, 13)
    key_base = jax.random.fold_in(key, 0)
    base = jax.random.normal(key_base, (2, C, 3 * C), jnp.float32) * C ** (-0.5)
    return base.astype(jnp.bfloat16)


def touch_ends(values, stream_key, smallest, largest):
    longest = values.shape.index(max(values.shape))
    spots = []
    for shift in (0, 1):
        where = [jax.random.randint(jax.random.fold_in(stream_key, axis), (), 0, length) for axis, length in enumerate(values.shape)]
        where[longest] = (where[longest] + shift) % values.shape[longest]
        spots.append(tuple(where))
    return values.at[spots[0]].set(smallest).at[spots[1]].set(largest)


def bell_draw(rng, dims, width, limit, kind=jnp.bfloat16):
    return jnp.clip(width * jax.random.normal(rng, dims, jnp.float32), -limit, limit).astype(kind)


def setup_inputs(seed: int = 0) -> dict:
    key_of = jax.random.split(jax.random.key(seed), 9)
    return {
        "field": draw_field(jax.random.fold_in(key_of[8], 71), 0),
        "shift": draw_shift(jax.random.fold_in(key_of[8], 71), 0),
        "window_type": touch_ends(jax.random.randint(key_of[2], (PL // WPL, NLATW), 0, TYPES), jax.random.fold_in(key_of[2], 1), 0, TYPES - 1).astype(jnp.int32),
        "qkv_weight": draw_qkv_weight(jax.random.fold_in(key_of[8], 71), 0),
        "proj_weight": bell_draw(key_of[4], (2, C, C), C ** -0.5, 0.4375),
        "up_weight": bell_draw(key_of[5], (2, C, FF_DIM), C ** -0.5, 0.4375),
        "down_weight": bell_draw(key_of[6], (2, FF_DIM, C), FF_DIM ** -0.5, 0.21875),
        "bias_table": bell_draw(key_of[7], (2, TYPES, HEADS, BIAS_LEN), 1.0, 4.0),
    }


def relative_index():
    lev_pos, lat_pos, lon_pos = np.meshgrid(np.arange(WPL), np.arange(WLAT), np.arange(WLON), indexing='ij')
    lev_pos = lev_pos.reshape(-1)
    lat_pos = lat_pos.reshape(-1)
    lon_pos = lon_pos.reshape(-1)
    level_pair = lev_pos[:, None] * WPL + lev_pos[None, :]
    lat_pair = lat_pos[:, None] * WLAT + lat_pos[None, :]
    lon_pair = lon_pos[:, None] - lon_pos[None, :] + WLON - 1
    return (level_pair * WLAT * WLAT + lat_pair) * (2 * WLON - 1) + lon_pair

def layer_norm(values, channels):
    shaped = values.astype(jnp.float32).reshape(values.shape[0], values.shape[1], -1, channels)
    center = shaped - lax.optimization_barrier(jnp.mean(shaped, axis=-1, keepdims=True))
    spread = lax.optimization_barrier(jnp.mean(center * center, axis=-1, keepdims=True))
    return (center * lax.rsqrt(spread + 1e-05)).reshape(values.shape)

def attend(region, band_ids, lat_label, level_label, qkv_w, proj_w, table, window_type):
    levels, row_count, merged = region.shape
    channels = proj_w.shape[0]
    lon_cells = merged // channels
    lev_win, lat_win, lon_win = (levels // WPL, row_count // WLAT, lon_cells // WLON)
    win_size = WPL * WLAT * WLON
    windows = region.reshape(lev_win, WPL, lat_win, WLAT, lon_win, WLON, channels)
    windows = windows.transpose(0, 2, 4, 1, 3, 5, 6).reshape(lev_win, lat_win, lon_win, win_size, channels)
    qkv_all = jnp.einsum('prwnc,cf->prwnf', windows.astype(jnp.float32), qkv_w.astype(jnp.float32)).astype(jnp.bfloat16)
    qkv_all = qkv_all.reshape(lev_win, lat_win, lon_win, win_size, 3, HEADS, HEAD_DIM)
    queries = qkv_all[:, :, :, :, 0].astype(jnp.float32)
    key_rows = qkv_all[:, :, :, :, 1].astype(jnp.float32)
    value_rows = qkv_all[:, :, :, :, 2].astype(jnp.float32)
    scores = jnp.einsum('prwnhd,prwmhd->prwhnm', queries, key_rows) * HEAD_DIM ** (-0.5)
    band_match = band_ids[:, None] == jnp.arange(window_type.shape[1])[None, :]
    types = lax.optimization_barrier(jnp.sum(jnp.where(band_match[None], window_type[:, None, :], 0), axis=-1))
    onehot = (types[..., None] == jnp.arange(table.shape[0])[None, None, :]).astype(jnp.float32)
    chosen = jnp.einsum('prt,thx->prhx', onehot, table.astype(jnp.float32))
    bias = chosen[..., relative_index()]
    scores = scores + bias[:, :, None]
    level_code = level_label.reshape(lev_win, WPL)
    lat_code = lat_label.reshape(lat_win, WLAT)
    code = level_code[:, None, :, None, None] * 2 + lat_code[None, :, None, :, None] + jnp.zeros((WLON,), jnp.int32)
    code = code.reshape(lev_win, lat_win, win_size)
    allowed = code[..., :, None] == code[..., None, :]
    scores = jnp.where(allowed[:, :, None, None], scores, -1e+30)
    peak = lax.optimization_barrier(jnp.max(scores, axis=-1, keepdims=True))
    expo = jnp.exp(scores - peak)
    probs = (expo / lax.optimization_barrier(jnp.sum(expo, axis=-1, keepdims=True))).astype(jnp.bfloat16)
    context = jnp.einsum('prwhnm,prwmhd->prwnhd', probs.astype(jnp.float32), value_rows).astype(jnp.bfloat16)
    context = context.reshape(lev_win, lat_win, lon_win, win_size, channels)
    mixed = jnp.einsum('prwnc,cf->prwnf', context.astype(jnp.float32), proj_w.astype(jnp.float32)).astype(jnp.bfloat16)
    mixed = mixed.reshape(lev_win, lat_win, lon_win, WPL, WLAT, WLON, channels)
    return mixed.transpose(0, 3, 1, 4, 2, 5, 6).reshape(levels, row_count, merged)

def banded(normed, lat_shift, lon_shift, level_shift, qkv_w, proj_w, table, window_type):
    rolled = jnp.roll(normed, -level_shift, axis=0)
    rolled = jnp.roll(rolled, -lat_shift, axis=1)
    rolled = jnp.roll(rolled, -lon_shift * C, axis=2)
    level_label = ((jnp.arange(PL) + level_shift) % PL < level_shift).astype(jnp.int32)

    def one_band(band):
        region = lax.dynamic_slice_in_dim(rolled, band * WLAT, WLAT, 1)
        orig_rows = (band * WLAT + jnp.arange(WLAT, dtype=jnp.int32) + lat_shift) % NLAT
        lat_label = (orig_rows < lat_shift).astype(jnp.int32)
        return attend(region, band[None], lat_label, level_label, qkv_w, proj_w, table, window_type)
    stacked = lax.map(one_band, jnp.arange(NLATW, dtype=jnp.int32))
    out = stacked.transpose(1, 0, 2, 3).reshape(PL, NLAT, NLON * C)
    out = jnp.roll(out, lon_shift * C, axis=2)
    out = jnp.roll(out, lat_shift, axis=1)
    return jnp.roll(out, level_shift, axis=0)

def feed_forward(field, attn, up_w, down_w):
    mixed = field.astype(jnp.float32) + attn.astype(jnp.float32)
    normed = layer_norm(mixed, C).astype(jnp.bfloat16).reshape(-1, C)
    hidden = jax.nn.gelu(jnp.dot(normed, up_w, preferred_element_type=jnp.float32), approximate=False).astype(jnp.bfloat16)
    result = mixed.reshape(-1, C) + jnp.dot(hidden, down_w, preferred_element_type=jnp.float32)
    return result.astype(jnp.bfloat16).reshape(field.shape)

def reference(field, shift, window_type, qkv_weight, proj_weight, up_weight, down_weight, bias_table):
    zero_shift = jnp.zeros((), jnp.int32)
    normed = layer_norm(field, C).astype(jnp.bfloat16)
    attn = banded(normed, zero_shift, zero_shift, 0, qkv_weight[0], proj_weight[0], bias_table[0], window_type)
    field_one = feed_forward(field, attn, up_weight[0], down_weight[0])
    normed = layer_norm(field_one, C).astype(jnp.bfloat16)
    attn = banded(normed, shift[0], shift[1], WPL // 2, qkv_weight[1], proj_weight[1], bias_table[1], window_type)
    return feed_forward(field_one, attn, up_weight[1], down_weight[1])
```

```python
import functools

import jax
import jax.numpy as jnp
import numpy as np
from jax import lax
from jax.experimental import pallas as pl
from jax.experimental.pallas import tpu as pltpu
from jax.sharding import PartitionSpec as P

HEADS = 6
HEAD_DIM = 32
C = 192
FF = 768
WPL = 2
WLAT = 6
WLON = 12
RP = 8
LEVELS = 4
SPAN = WLAT * (2 * WLON - 1)
NEG = -1e30
LOG2E = 1.4426950408889634
F32 = jnp.float32
BF = jnp.bfloat16


def mm(a, b):
    return jnp.dot(a, b, preferred_element_type=F32)


def mm_nt(a, b):
    return lax.dot_general(a, b, (((1,), (1,)), ((), ())), preferred_element_type=F32)


def norm(x):
    center = x - jnp.mean(x, axis=-1, keepdims=True)
    spread = jnp.mean(center * center, axis=-1, keepdims=True)
    return center * lax.rsqrt(spread + 1e-05)


def gelu(x):
    return 0.5 * x * (1.0 + lax.erf(x * 0.7071067811865476))


def iota(shape, dim):
    return lax.broadcasted_iota(jnp.int32, shape, dim)


def head_mask(h, dtype):
    lane = iota((1, C), 1)
    return ((lane >= h * HEAD_DIM) & (lane < (h + 1) * HEAD_DIM)).astype(dtype)


def bias_kernel(block, wt, sh, dev, *refs):
    bands = 2 if block else 1
    tabs, out_ref, cut = refs[: 2 * bands], refs[2 * bands], refs[2 * bands + 1]
    t = sh[0] if block else 0
    cut[...] = jnp.zeros_like(cut)
    for k in range(2 * bands):
        tab = tabs[k][0, 0].astype(F32)
        for p1 in range(WPL):
            for p2 in range(WPL):
                for i1 in range(WLAT):
                    a = ((p1 * WPL + p2) * WLAT + i1) * SPAN
                    row = (p1 * WLAT + i1) * 8
                    cut[k, p2, row : row + HEADS, :] = tab[:, a : a + SPAN]
    n = HEADS * WPL * RP
    o, s = iota((n, n), 0), iota((n, n), 1)
    r1 = o & 7
    i1 = jnp.where(r1 >= t, r1 - t, r1 - t + WLAT)
    want = (((o >> 3) & 1) * WLAT + i1) * 8 + (o >> 4)
    hit = (s == want) & (r1 < WLAT)
    picks = [hit & (r1 >= t), hit & (r1 < t)] if block else [hit]
    picks = [p.astype(F32).astype(BF) for p in picks]
    left = []
    for p2 in range(WPL):
        parts = []
        for lw in range(2):
            acc = mm(picks[0], cut[lw * bands, p2].astype(BF))
            if block:
                acc = acc + mm(picks[1], cut[lw * bands + 1, p2].astype(BF))
            parts.append(acc)
        left.append(jnp.concatenate(parts, axis=0).astype(BF))
    m = iota((1, C), 1)
    p2m = (m >= WLON * RP).astype(jnp.int32)
    r2 = m & 7
    j2 = (m >> 3) - p2m * WLON
    i2 = jnp.where(r2 >= t, r2 - t, r2 - t + WLAT)
    place = i2 * (2 * WLON - 1) + (WLON - 1) - j2
    rows, cols = iota((2 * n, C), 0), iota((2 * n, C), 1)
    kr, qr = cols & 7, rows & 7
    dead = kr >= WLAT
    if block:
        kp = (cols >= WLON * RP).astype(jnp.int32)
        dead = dead | ((rows >= n) & (((rows >> 3) & 1) != kp))
        a = dev[0]
        edge = ((qr >= t) & (a == dev[1] - 1)) | ((qr < t) & (a == 0))
        dead = dead | (edge & ((qr < t) != (kr < t)))
    mask = jnp.where(dead, NEG, 0.0).astype(F32)
    k = iota((SPAN, C), 0)
    for j1 in range(WLON):
        acc = mask
        for p2 in range(WPL):
            target = jnp.where((p2m == p2) & (r2 < WLAT), place + j1, -1)
            pick = (k == target).astype(F32).astype(BF)
            acc = acc + mm(left[p2], pick) * LOG2E
        out_ref[:, :, :, j1] = acc.reshape(2, HEADS, WPL, RP, C)


def bias_call(block, wt, sh, dev, table):
    bands = 2 if block else 1
    specs = []
    for lw in range(2):
        for north in range(bands):
            specs.append(
                pl.BlockSpec(
                    (1, 1, HEADS, table.shape[-1]),
                    lambda i, wt, sh, dev, lw=lw, north=north: (
                        block,
                        wt[lw, (dev[0] + dev[1] - north) % dev[1]],
                        0,
                        0,
                    ),
                )
            )
    shape = (2, HEADS, WPL, WLON, RP, C)
    return pl.pallas_call(
        functools.partial(bias_kernel, block),
        out_shape=jax.ShapeDtypeStruct(shape, F32),
        grid_spec=pltpu.PrefetchScalarGridSpec(
            num_scalar_prefetch=3,
            grid=(1,),
            in_specs=specs,
            out_specs=pl.BlockSpec(shape, lambda i, *_: (0,) * 6),
            scratch_shapes=[pltpu.VMEM((2 * bands, WPL, 12 * 8, SPAN), F32)],
        ),
        compiler_params=pltpu.CompilerParams(vmem_limit_bytes=48 * 2**20),
        cost_estimate=pl.CostEstimate(flops=10**9, bytes_accessed=4 * 10**6, transcendentals=0),
        name=f"bias{block}",
    )(wt, sh, dev, *([table] * (2 * bands)))


def ffn(mid, up, down):
    h_in = norm(mid).astype(BF)
    out = mid
    for f in range(0, FF, 256):
        hid = gelu(mm(h_in, up[0, :, f : f + 256])).astype(BF)
        out = out + mm(hid, down[0, f : f + 256, :])
    return out.astype(BF).astype(F32)


def softmax_rows(scores, bias):
    z = scores + bias
    return jnp.exp2(z - jnp.max(z, axis=-1, keepdims=True)).astype(BF)


def rows2(ref, stride, la, lb, start, count):
    return jnp.concatenate(
        [ref[la * stride + start : la * stride + start + count, :],
         ref[lb * stride + start : lb * stride + start + count, :]], axis=0)


WIN = WLON * RP


def block0(load, cells, bias, wqkv, wproj, up, down, x_s, q_s, k_s, v_s, a_s):
    x_s[...] = jnp.zeros_like(x_s)
    for l in range(LEVELS):
        for c in range(cells):
            x_s[l, c, 0:WLAT, :] = load(l, c)
    n = cells * RP
    wq, wk, wv = (wqkv[0, :, i * C : (i + 1) * C] for i in range(3))
    for l in range(LEVELS):
        xn = norm(x_s[l].reshape(n, C)).astype(BF)
        q_s[l * n : (l + 1) * n, :] = (mm(xn, wq) * (HEAD_DIM**-0.5 * LOG2E)).astype(BF)
        k_s[l * n : (l + 1) * n, :] = mm(xn, wk).astype(BF)
        v_s[l * n : (l + 1) * n, :] = mm(xn, wv).astype(BF)
    ones = [jnp.broadcast_to(head_mask(h, BF), (2 * WIN, C)) for h in range(HEADS)]
    for lw in range(2):
        for w in range(cells // WLON):
            la, lb = 2 * lw, 2 * lw + 1
            q = rows2(q_s, n, la, lb, w * WIN, WIN)
            k = rows2(k_s, n, la, lb, w * WIN, WIN)
            v = rows2(v_s, n, la, lb, w * WIN, WIN)
            qs = jnp.concatenate([q * head_mask(h, BF) for h in range(HEADS)], axis=0)
            scores = mm_nt(qs, k)
            acc = jnp.zeros((2 * WIN, C), F32)
            den = jnp.zeros((2 * WIN, C), F32)
            for h in range(HEADS):
                p = softmax_rows(
                    scores[h * 2 * WIN : (h + 1) * 2 * WIN], bias[lw, h].reshape(2 * WIN, C)
                )
                acc = acc + mm(p, v * head_mask(h, BF))
                den = den + mm(p, ones[h])
            att = mm((acc / den).astype(BF), wproj[0])
            a_s[la, w * WLON : (w + 1) * WLON] = att[:WIN].reshape(WLON, RP, C)
            a_s[lb, w * WLON : (w + 1) * WLON] = att[WIN:].reshape(WLON, RP, C)
    outs = []
    for l in range(LEVELS):
        outs.append(ffn((x_s[l] + a_s[l]).reshape(n, C), up, down))
    return outs


def tile_kernel(x, bias, wqkv, wproj, up, down, f_ref, n_ref, x_s, q_s, k_s, v_s, a_s):
    cells = x_s.shape[1]
    load = lambda l, c: x[l, :, c * C : (c + 1) * C].astype(F32)
    outs = block0(load, cells, bias, wqkv, wproj, up, down, x_s, q_s, k_s, v_s, a_s)
    for l in range(LEVELS):
        f_ref[l] = outs[l].reshape(cells, RP, C)
        n_ref[l] = norm(outs[l]).reshape(cells, RP, C)


GROUP = 16 * RP
PACKED = 16 * 5


def pack_matrix(first):
    m = np.zeros((PACKED, GROUP), np.float32)
    free = [s for s in range(RP) if not first <= s < first + 5]
    for g in range(2):
        for i in range(5):
            for s in range(RP):
                if s in free:
                    src = (5 + free.index(s)) * RP + first + i
                else:
                    src = i * RP + s
                m[g * 40 + i * RP + s, g * 64 + src] = 1
    return m


def split_point(rows):
    return (rows // 2 + 15) // 16 * 16


def pack(full, matrix):
    rows = full.shape[0] // GROUP * PACKED
    parts = [mm(matrix, full[g : g + GROUP]) for g in range(0, full.shape[0], GROUP)]
    y = jnp.concatenate(parts, axis=0)
    half = split_point(rows)
    tail = jnp.concatenate([y[half:, 128:], jnp.zeros((2 * half - rows, 64), F32)], axis=0)
    return jnp.concatenate(
        [y[:, :128], jnp.concatenate([y[:half, 128:], tail], axis=1)], axis=0
    ).astype(BF)


def unpack(data, matrix, rows):
    half = data.shape[0] - rows
    high = jnp.concatenate(
        [data[rows:, :64].astype(F32), data[rows : 2 * rows - half, 64:].astype(F32)], axis=0
    ).astype(BF)
    parts = []
    for g in range(0, rows, PACKED):
        parts.append(
            jnp.concatenate(
                [mm(matrix, data[g : g + PACKED]), mm(matrix, high[g : g + PACKED])], axis=1
            )
        )
    return jnp.concatenate(parts, axis=0)


def edge_kernel(
    east, west, own, bias, wqkv, wproj, up, down, pup, pdn,
    ext_ref, up_ref, dn_ref, x_s, q_s, k_s, v_s, a_s,
):
    cells = x_s.shape[1]

    def load(l, c):
        ref = east if c < WLON else west
        c = c % WLON
        return ref[l, :, c * C : (c + 1) * C].astype(F32)

    outs = block0(load, cells, bias, wqkv, wproj, up, down, x_s, q_s, k_s, v_s, a_s)
    full = []
    for l in range(LEVELS):
        side = norm(outs[l]).reshape(cells, RP, C)
        row = jnp.concatenate([side[cells - 1 :], own[l], side[: WLON - 1]], axis=0)
        ext_ref[l] = row
        full.append(row.reshape(-1, C))
    full = jnp.concatenate(full, axis=0).astype(BF)
    up_ref[...] = pack(full, pup[...])
    dn_ref[...] = pack(full, pdn[...])


def shifted_kernel(
    sh, f1, ext, above, below, bias, wqkv, wproj, up, down, uup, udn,
    out, ks_s, vs_s, kn_s, vn_s, qs_s, qn_s, a_s, sc_s,
):
    t = sh[0]
    cells = f1.shape[1]
    wide = ext.shape[1]
    n, m = cells * RP, wide * RP
    wq, wk, wv = (wqkv[0, :, i * C : (i + 1) * C] for i in range(3))
    packed = LEVELS * m // GROUP * PACKED
    north = unpack(above[...], udn[...], packed)
    south = unpack(below[...], uup[...], packed)
    row = iota((m, 1), 0) & 7
    for l in range(LEVELS):
        mine = ext[l].reshape(m, C)
        xs = jnp.where(row >= t, mine, south[l * m : (l + 1) * m]).astype(BF)
        xn = jnp.where(row < t, mine, north[l * m : (l + 1) * m]).astype(BF)
        ks_s[l * m : (l + 1) * m, :] = mm(xs, wk).astype(BF)
        vs_s[l * m : (l + 1) * m, :] = mm(xs, wv).astype(BF)
        kn_s[l * m : (l + 1) * m, :] = mm(xn, wk).astype(BF)
        vn_s[l * m : (l + 1) * m, :] = mm(xn, wv).astype(BF)
        mine = jnp.concatenate([ext[l, cells : cells + 1], ext[l, 1:cells]], axis=0)
        q = mm(mine.reshape(n, C).astype(BF), wq) * (HEAD_DIM**-0.5 * LOG2E)
        qs_s[l * n : (l + 1) * n, :] = jnp.where(row[:n] >= t, q, 0.0).astype(BF)
        qn_s[l * n : (l + 1) * n, :] = jnp.where(row[:n] < t, q, 0.0).astype(BF)
    ones = [jnp.broadcast_to(head_mask(h, BF), (2 * WIN, C)) for h in range(HEADS)]
    lo = (iota((2 * WIN, 1), 0) & 7) >= t
    lo_edge = lo[: 2 * RP]
    for lw in range(2):
        la, lb = (2 * lw + 1) % LEVELS, (2 * lw + 2) % LEVELS
        for w in range(cells // WLON):
            qs = rows2(qs_s, n, la, lb, w * WIN, WIN)
            qn = rows2(qn_s, n, la, lb, w * WIN, WIN)
            pick = lambda ref, at: rows2(ref, m, la, lb, at * WIN, WIN)
            stack = lambda q: jnp.concatenate([q * head_mask(h, BF) for h in range(HEADS)], axis=0)
            scores = mm_nt(stack(qs), pick(ks_s, w)) + mm_nt(stack(qn), pick(kn_s, w))
            sc_s[...] = scores.reshape(HEADS, WPL, WLON, RP, C)
            vs, vn = pick(vs_s, w), pick(vn_s, w)
            if w == 0:
                last = cells // WLON
                first = lambda ref: jnp.concatenate(
                    [ref[la * n : la * n + 16, :].astype(F32)[:RP],
                     ref[lb * n : lb * n + 16, :].astype(F32)[:RP]], axis=0).astype(BF)
                edge = mm_nt(stack(first(qs_s)), pick(ks_s, last)) + mm_nt(
                    stack(first(qn_s)), pick(kn_s, last))
                sc_s[:, :, 0] = edge.reshape(HEADS, WPL, RP, C)
                vs2, vn2 = pick(vs_s, last), pick(vn_s, last)
                acc_s2 = jnp.zeros((2 * RP, C), F32)
                acc_n2 = jnp.zeros((2 * RP, C), F32)
            acc_s = jnp.zeros((2 * WIN, C), F32)
            acc_n = jnp.zeros((2 * WIN, C), F32)
            den = jnp.zeros((2 * WIN, C), F32)
            for h in range(HEADS):
                z = sc_s[h].reshape(2 * WIN, C) + bias[lw, h].reshape(2 * WIN, C)
                e = jnp.exp2(z - jnp.max(z, axis=-1, keepdims=True))
                p = e.astype(BF)
                hm = head_mask(h, BF)
                acc_s = acc_s + mm(p, vs * hm)
                acc_n = acc_n + mm(p, vn * hm)
                den = den + mm(p, ones[h])
                if w == 0:
                    p2 = e.reshape(WPL, WLON, RP, C)[:, 0].reshape(2 * RP, C).astype(BF)
                    acc_s2 = acc_s2 + mm(p2, vs2 * hm)
                    acc_n2 = acc_n2 + mm(p2, vn2 * hm)
            acc = jnp.where(lo, acc_s, acc_n)
            if w == 0:
                fix = jnp.where(lo_edge, acc_s2, acc_n2)
                acc = jnp.concatenate(
                    [fix[:RP], acc[RP:WIN], fix[RP:], acc[WIN + RP :]], axis=0)
            att = mm((acc / den).astype(BF), wproj[0])
            a_s[la, w * WLON : (w + 1) * WLON] = att[:WIN].reshape(WLON, RP, C)
            a_s[lb, w * WLON : (w + 1) * WLON] = att[WIN:].reshape(WLON, RP, C)
    for l in range(LEVELS):
        base = jnp.concatenate([f1[l, cells - 1 :], f1[l, : cells - 1]], axis=0)
        res = ffn((base + a_s[l]).reshape(n, C), up, down).reshape(cells, RP, C)
        for c in range(0, cells, 2):
            pair = jnp.concatenate([res[(c + 1) % cells], res[(c + 2) % cells]], axis=1)
            out[l, :, c * C : (c + 2) * C] = pair[:WLAT].astype(BF)


def weight_specs(block):
    pick = lambda i, *_: (block, 0, 0)
    return [
        pl.BlockSpec((1, C, 3 * C), pick),
        pl.BlockSpec((1, C, C), pick),
        pl.BlockSpec((1, C, FF), pick),
        pl.BlockSpec((1, FF, C), pick),
    ]


def full_spec(shape):
    return pl.BlockSpec(shape, lambda i, *_: (0,) * len(shape))


def call(kernel, block, args, weights, extra, outs, scratch, prefetch=(), flops=10**9, name=None):
    return pl.pallas_call(
        kernel,
        out_shape=outs,
        grid_spec=pltpu.PrefetchScalarGridSpec(
            num_scalar_prefetch=len(prefetch),
            grid=(1,),
            in_specs=[full_spec(a.shape) for a in args]
            + weight_specs(block)
            + [full_spec(a.shape) for a in extra],
            out_specs=[full_spec(o.shape) for o in outs],
            scratch_shapes=scratch,
        ),
        compiler_params=pltpu.CompilerParams(vmem_limit_bytes=48 * 2**20),
        cost_estimate=pl.CostEstimate(
            flops=flops, bytes_accessed=6 * 10**6, transcendentals=10**6
        ),
        name=name,
    )(*prefetch, *args, *weights, *extra)


def shifted(x, axis, by):
    size = lax.axis_size(axis)
    return lax.ppermute(x, axis, [(i, (i + by) % size) for i in range(size)])


def body(field, shift, window_type, qkv_weight, proj_weight, up_weight, down_weight, bias_table):
    cells = field.shape[2] // C
    wide = cells + WLON
    half = WLON * C
    weights = (qkv_weight, proj_weight, up_weight, down_weight)
    dev = jnp.stack([lax.axis_index("lat"), jnp.int32(lax.axis_size("lat"))]).astype(jnp.int32)
    east = shifted(field[:, :, :half], "lon", -1)
    west = shifted(field[:, :, (cells - WLON) * C :], "lon", 1)
    bias0 = bias_call(0, window_type, shift, dev, bias_table)

    def sds(shape, dtype):
        return jax.ShapeDtypeStruct(shape, dtype)

    def scratch0(cells):
        n = LEVELS * cells * RP
        return [pltpu.VMEM((LEVELS, cells, RP, C), F32)] + [pltpu.VMEM((n, C), BF)] * 3 + [
            pltpu.VMEM((LEVELS, cells, RP, C), F32)]

    tile = (LEVELS, cells, RP, C)
    f1, n1 = call(
        tile_kernel, 0, (field, bias0), weights, (),
        [sds(tile, F32), sds(tile, F32)], scratch0(cells), name="tile0")
    rows = LEVELS * wide * RP // GROUP * PACKED
    pay = (rows + split_point(rows), 128)
    mup, mdn = pack_matrix(0), pack_matrix(1)
    ext, pay_up, pay_dn = call(
        edge_kernel, 0, (east, west, n1, bias0), weights,
        (jnp.asarray(mup, BF), jnp.asarray(mdn, BF)),
        [sds((LEVELS, wide, RP, C), F32), sds(pay, BF), sds(pay, BF)],
        scratch0(2 * WLON), name="edge0")
    below = shifted(pay_up, "lat", -1)
    above = shifted(pay_dn, "lat", 1)
    bias1 = bias_call(1, window_type, shift, dev, bias_table)
    n, m = LEVELS * cells * RP, LEVELS * wide * RP
    (out,) = call(
        shifted_kernel, 1, (f1, ext, above, below, bias1), weights,
        (jnp.asarray(mup.T, BF), jnp.asarray(mdn.T, BF)),
        [sds(field.shape, BF)],
        [pltpu.VMEM((m, C), BF)] * 4 + [pltpu.VMEM((n, C), BF)] * 2
        + [pltpu.VMEM(tile, F32), pltpu.VMEM((HEADS, WPL, WLON, RP, C), F32)],
        prefetch=(shift,), name="tile1")
    return out


def solution(mesh):
    return jax.shard_map(
        body,
        mesh=mesh,
        in_specs=(P(None, "lat", "lon"), P(), P(), P(), P(), P(), P(), P()),
        out_specs=P(None, "lat", "lon"),
        check_vma=False,
    )
```

```python
import functools

import jax
import jax.numpy as jnp
from jax import lax
from jax.experimental import pallas as pl
from jax.experimental.pallas import tpu as pltpu
from jax.sharding import PartitionSpec as P


HEADS = 6
HEAD_DIM = 32
C = 192
FF = 768
WLAT = 6
WLON = 12
TILE = 8
PAIRS = WLON // 2
RPS = WLAT // 2
COL = RPS * TILE
WIN = PAIRS * COL
SPAN = WLAT * (2 * WLON - 1)
NEG = -1e30
LOG2E = 1.4426950408889634
F32 = jnp.float32
BF = jnp.bfloat16


def mm(a, b):
    return jnp.dot(a, b, preferred_element_type=F32)


def mm_nt(a, b):
    return lax.dot_general(a, b, (((1,), (1,)), ((), ())), preferred_element_type=F32)


def norm(x, short):
    ones = jnp.ones((C, C), BF)
    high = x.astype(BF)
    total = mm(high, ones)
    if not short:
        total = total + mm((x - high.astype(F32)).astype(BF), ones)
    center = x - total * (1.0 / C)
    spread = mm((center * center).astype(BF), ones) * (1.0 / C)
    return center * lax.rsqrt(spread + 1e-05)


def gelu(x):
    return 0.5 * x * (1.0 + lax.erf(x * 0.7071067811865476))


def iota(shape, dim):
    return lax.broadcasted_iota(jnp.int32, shape, dim)


def head_mask(h):
    lane = iota((1, C), 1)
    return ((lane >= h * HEAD_DIM) & (lane < (h + 1) * HEAD_DIM)).astype(F32).astype(BF)


WIDE = 256


def value_mask(h):
    lane = iota((1, WIDE), 1)
    hit = (lane >= h * HEAD_DIM) & (lane < (h + 1) * HEAD_DIM) | (lane == C + h)
    if h == 0:
        hit = hit | (lane >= C + HEADS)
    return hit.astype(F32).astype(BF)


def divide(acc):
    tail = acc[:, 128:]
    inv = 1.0 / jnp.where(iota((1, 128), 1) >= 64, tail, 1.0)
    high = inv.astype(BF)
    low = (inv - high.astype(F32)).astype(BF)
    i, lane = iota((128, C), 0), iota((128, C), 1)
    first = (i - 64) * HEAD_DIM
    spread = ((lane >= first) & (lane < first + HEAD_DIM)).astype(F32).astype(BF)
    return (acc[:, :C] * (mm(high, spread) + mm(low, spread))).astype(BF)


def stack_heads(q):
    return jnp.concatenate([q * head_mask(h) for h in range(HEADS)], axis=0)


def tile_bits(shape, dim):
    s = iota(shape, dim)
    return s >> 2, (s >> 1) & 1, s & 1


def bias_kernel(block, wt, sh, dev, tab, out_ref, cut):
    t = sh[0] if block else 0
    lat, lats = dev[0], dev[1]
    for h in range(HEADS):
        rows = tab[block, h].astype(F32)
        for p1 in range(2):
            for p2 in range(2):
                for i1 in range(WLAT):
                    a = ((p1 * 2 + p2) * WLAT + i1) * SPAN
                    at = (p1 * WLAT + i1) * 16
                    cut[h, p2, at : at + 16, :] = rows[:, a : a + SPAN].astype(BF)
    n, src = 2 * COL, 2 * WLAT * 16
    o, s = iota((n, src), 0), iota((n, src), 1)
    lw = (o >= COL).astype(jnp.int32)
    q = o - COL * lw
    r1 = 2 * (q >> 3) + ((q >> 2) & 1)
    p1 = (q & 1) ^ block
    own = r1 >= t
    i1 = jnp.where(own, r1 - t, r1 - t + WLAT)
    north = lax.rem(lat + lats - 1, lats)
    kind = jnp.where(
        lw == 0,
        jnp.where(own, wt[0, lat], wt[0, north]),
        jnp.where(own, wt[1, lat], wt[1, north]),
    )
    hit = s == (p1 * WLAT + i1) * 16 + kind
    cell = (q >> 1) & 1
    picks = [(hit & (cell == b)).astype(F32).astype(BF) for b in range(2)]
    pick2 = jnp.concatenate(picks, axis=0)
    left = [[[], []], [[], []]]
    for p2 in range(2):
        for h in range(HEADS):
            both = mm(pick2, cut[h, p2]).astype(BF)
            for b in range(2):
                left[b][p2].append(both[b * n : (b + 1) * n])
    left = [[jnp.concatenate(x, axis=0) for x in y] for y in left]
    m = iota((1, WIN), 1)
    cp2 = (m * 171) >> 12
    u = m - cp2 * COL
    r2 = 2 * (u >> 3) + ((u >> 2) & 1)
    j2 = 2 * cp2 + (((u >> 1) & 1) ^ block)
    p2m = (u & 1) ^ block
    i2 = jnp.where(r2 >= t, r2 - t, r2 - t + WLAT)
    place = i2 * (2 * WLON - 1) + (WLON - 1) - j2
    k = iota((SPAN, WIN), 0)
    mask = None
    if block:
        o = iota((n, WIN), 0)
        lw = (o >= COL).astype(jnp.int32)
        q = o - COL * lw
        r1 = 2 * (q >> 3) + ((q >> 2) & 1)
        south = r1 >= t
        edge = (south & (lat == lats - 1)) | (~south & (lat == 0))
        dead = (lw == 1) & (((q & 1) ^ block) != p2m)
        dead = dead | (edge & ((r1 < t) != (r2 < t)))
        mask = jnp.where(dead, NEG, 0.0).astype(F32)
        mask = jnp.concatenate([mask] * HEADS, axis=0)
    for cp1 in range(PAIRS):
        acc = None
        for b in range(2):
            j1 = 2 * cp1 + (b ^ block)
            for p2 in range(2):
                target = jnp.where(p2m == p2, place + j1, -1)
                pick = (k == target).astype(F32).astype(BF)
                term = mm(left[b][p2], pick)
                acc = term if acc is None else acc + term
        acc = acc * LOG2E
        if block:
            acc = acc + mask
        for h in range(HEADS):
            for lw in range(2):
                out_ref[lw, h, cp1] = acc[(2 * h + lw) * COL : (2 * h + lw + 1) * COL]


VM = pl.BlockSpec(memory_space=pltpu.VMEM)
SM = pl.BlockSpec(memory_space=pltpu.SMEM)


def bias_call(block, wt, sh, dev, table):
    return pl.pallas_call(
        functools.partial(bias_kernel, block),
        out_shape=jax.ShapeDtypeStruct((2, HEADS, PAIRS, COL, WIN), F32),
        in_specs=[SM, SM, SM, VM],
        out_specs=VM,
        scratch_shapes=[pltpu.VMEM((HEADS, 2, 2 * WLAT * 16, SPAN), BF)],
        compiler_params=pltpu.CompilerParams(vmem_limit_bytes=24 * 2**20),
        cost_estimate=pl.CostEstimate(flops=10**9, bytes_accessed=4 * 10**6, transcendentals=0),
        name=f"bias{block}",
    )(wt, sh, dev, table)


def ffn(block, mid, up, down):
    h_in = norm(mid, False).astype(BF)
    out = mid
    for f in range(0, FF, 256):
        hid = gelu(mm(h_in, up[block, :, f : f + 256])).astype(BF)
        out = out + mm_nt(hid, down[block, :, f : f + 256])
    return out.astype(BF).astype(F32)


def weights_of(z):
    return jnp.exp2(z - jnp.max(z, axis=-1, keepdims=True)).astype(BF)


def split_point(rows):
    return (rows // 2 + 15) // 16 * 16


def fold(y):
    rows = y.shape[0]
    half = split_point(rows)
    tail = jnp.concatenate([y[half:, 128:], jnp.zeros((2 * half - rows, 64), F32)], axis=0)
    high = jnp.concatenate([y[:half, 128:], tail], axis=1)
    return jnp.concatenate([y[:, :128], high], axis=0).astype(BF)


def unfold(data, rows):
    half = data.shape[0] - rows
    data = data.astype(F32)
    high = jnp.concatenate([data[rows:, :64], data[rows : 2 * rows - half, 64:]], axis=0)
    return jnp.concatenate([data[:rows], high], axis=1)


def tiles_of(ref, rp, k):
    two = jnp.concatenate(
        [ref[2 * rp + d, :, 2 * k * C : 2 * (k + 1) * C].astype(F32) for d in range(2)], axis=0
    )
    a, b = two[:, :C], two[:, C:]
    low = (iota((TILE, 1), 0) & 3) < 2
    return jnp.where(low, a, pltpu.roll(b, 2, 0)), jnp.where(low, pltpu.roll(a, 6, 0), b)


def first_kernel(
    x, east, west, bias, wqkv, wproj, up, down,
    f_ref, ext_ref, up_ref, dn_ref, x_s, f_s, q_s, k_s, v_s,
):
    own = x.shape[2] // C // 2
    cps = x_s.shape[1]
    for cp in range(cps):
        ref, k = (x, cp) if cp < own else ((east, cp - own) if cp < own + PAIRS else (west, cp - own - PAIRS))
        for rp in range(RPS):
            x_s[0, cp, rp], x_s[1, cp, rp] = tiles_of(ref, rp, k)
    rows = cps * COL
    wins = cps // PAIRS
    wq, wk, wv = (wqkv[0, :, i * C : (i + 1) * C] for i in range(3))
    for lw in range(2):
        for i in range(wins):
            at = lw * rows + i * WIN
            xn = norm(x_s[lw, i * PAIRS : (i + 1) * PAIRS].reshape(WIN, C), True).astype(BF)
            q_s[at : at + WIN, :] = (mm(xn, wq) * (HEAD_DIM**-0.5 * LOG2E)).astype(BF)
            k_s[at : at + WIN, :] = mm(xn, wk).astype(BF)
            v_s[at : at + WIN, :C] = mm(xn, wv).astype(BF)
    v_s[:, C:] = jnp.ones((2 * rows, WIDE - C), BF)

    def attend(lw, i, skip):
        at = lw * rows + i * WIN
        n = WIN - skip * COL
        q = q_s[at : at + WIN, :].astype(F32)[skip * COL :].astype(BF)
        scores = mm_nt(stack_heads(q), k_s[at : at + WIN, :])
        v = v_s[at : at + WIN, :]
        acc = None
        for h in range(HEADS):
            b = bias[lw, h, skip:].reshape(n, WIN)
            term = mm(weights_of(scores[h * n : (h + 1) * n] + b), v * value_mask(h))
            acc = term if acc is None else acc + term
        return mm(divide(acc), wproj[0])

    west_at = own + PAIRS
    for lw in range(2):
        for i in range(wins - 1):
            sl = slice(i * PAIRS, (i + 1) * PAIRS)
            mid = x_s[lw, sl].reshape(WIN, C) + attend(lw, i, 0)
            f_s[lw, sl] = mid.reshape(PAIRS, RPS, TILE, C)
        mid = x_s[lw, cps - 1].reshape(COL, C) + attend(lw, wins - 1, PAIRS - 1)
        f_s[lw, west_at] = mid.reshape(RPS, TILE, C)
        res = ffn(0, f_s[lw].reshape(-1, C), up, down)
        f_s[lw] = res.reshape(west_at + 1, RPS, TILE, C)
    _, cell, level = tile_bits((1, 1, TILE, 1), 2)
    keep = [level == 1, level == 0]
    for w in range(2):
        pick = lambda sl: jnp.where(keep[w], f_s[0, sl], f_s[1, sl])
        mine = pick(slice(0, own))
        before = jnp.concatenate([mine[own - 1 :], mine[: own - 1]], axis=0)
        f_ref[w] = jnp.where(cell == 0, mine, before)
        o = jnp.concatenate(
            [pick(slice(west_at, west_at + 1)), mine, pick(slice(own, own + PAIRS))], axis=0)
        o = norm(o.reshape(-1, C), True).reshape(o.shape)
        ext_ref[w] = jnp.where(cell == 0, o[1:], o[:-1])
    e = [ext_ref[w] for w in range(2)]
    top = (iota((1, TILE, 1), 1)) < 4
    flat = lambda a: a.reshape(-1, C)
    roll4 = lambda a: pltpu.roll(a, 4, 1)
    half = jnp.where(top, e[0][:, 2], roll4(e[1][:, 2]))
    up_ref[...] = fold(jnp.concatenate([flat(e[0][:, :2]), flat(e[1][:, :2]), flat(half)], axis=0))
    half = jnp.where(top, roll4(e[1][:, 0]), e[0][:, 0])
    dn_ref[...] = fold(jnp.concatenate([flat(e[0][:, 1:]), flat(e[1][:, 1:]), flat(half)], axis=0))


def second_kernel(
    sh, f1, ext, above, below, bias, wqkv, wproj, up, down,
    out, ks_s, vs_s, kn_s, vn_s, qs_s, qn_s, r_s,
):
    t = sh[0]
    own, wide = f1.shape[1], ext.shape[1]
    wq, wk, wv = (wqkv[1, :, i * C : (i + 1) * C] for i in range(3))
    packed = 2 * wide * 20
    south = unfold(below[...], packed)
    north = unfold(above[...], packed)
    full = wide * 16
    roll4 = lambda a: pltpu.roll(a, 4, 1)

    def halves(y):
        rest = y[2 * full :].reshape(wide, TILE, C)
        return [y[w * full : (w + 1) * full].reshape(wide, 2, TILE, C) for w in range(2)], rest

    (s_full, s_half), (n_full, n_half) = halves(south), halves(north)
    shape = (1, RPS, TILE, 1)
    row_bit, cell, level = tile_bits(shape, 2)
    row = 2 * iota(shape, 1) + row_bit
    lower = row >= t
    tiles = lambda a: a.reshape(PAIRS, RPS, TILE, C)
    for w in range(2):
        sh_half = (s_half if w == 0 else roll4(s_half))[:, None]
        nh_half = (roll4(n_half) if w else n_half)[:, None]
        for i in range(wide // PAIRS):
            sl = slice(i * PAIRS, (i + 1) * PAIRS)
            at = w * wide * COL + i * WIN
            mine = ext[w, sl]
            below_t = jnp.concatenate([s_full[w][sl], sh_half[sl]], axis=1)
            above_t = jnp.concatenate([nh_half[sl], n_full[w][sl]], axis=1)
            xs = jnp.where(lower, mine, below_t).reshape(WIN, C).astype(BF)
            xn = jnp.where(lower, above_t, mine).reshape(WIN, C).astype(BF)
            ks_s[at : at + WIN, :] = mm(xs, wk).astype(BF)
            vs_s[at : at + WIN, :C] = mm(xs, wv).astype(BF)
            kn_s[at : at + WIN, :] = mm(xn, wk).astype(BF)
            vn_s[at : at + WIN, :C] = mm(xn, wv).astype(BF)
        for i in range(own // PAIRS):
            sl = slice(i * PAIRS, (i + 1) * PAIRS)
            at = w * own * COL + i * WIN
            mine = ext[w, sl]
            if i == 0:
                fix = jnp.where(cell == 0, mine[:1], ext[w, own : own + 1])
                mine = jnp.concatenate([fix, mine[1:]], axis=0)
            q = mm(mine.reshape(WIN, C).astype(BF), wq) * (HEAD_DIM**-0.5 * LOG2E)
            q = tiles(q)
            qs_s[at : at + WIN, :] = jnp.where(lower, q, 0.0).reshape(WIN, C).astype(BF)
            qn_s[at : at + WIN, :] = jnp.where(lower, 0.0, q).reshape(WIN, C).astype(BF)
    vs_s[:, C:] = vn_s[:, C:] = jnp.ones((2 * wide * COL, WIDE - C), BF)
    late = ((iota((COL, 1), 0) >> 1) & 1) == 1
    last = own // PAIRS
    for w in range(2):
        for i in range(own // PAIRS):
            qs = qs_s[w * own * COL + i * WIN : w * own * COL + (i + 1) * WIN, :]
            qn = qn_s[w * own * COL + i * WIN : w * own * COL + (i + 1) * WIN, :]
            pick = lambda ref, j: ref[
                w * wide * COL + j * WIN : w * wide * COL + (j + 1) * WIN, :]
            scores = mm_nt(stack_heads(qs), pick(ks_s, i)) + mm_nt(stack_heads(qn), pick(kn_s, i))
            vs, vn = pick(vs_s, i), pick(vn_s, i)
            if i == 0:
                first = lambda q: q.astype(F32)[:COL].astype(BF)
                edge = mm_nt(stack_heads(first(qs)), pick(ks_s, last)) + mm_nt(
                    stack_heads(first(qn)), pick(kn_s, last))
                vs2, vn2 = pick(vs_s, last), pick(vn_s, last)
                fix_s, fix_n = jnp.zeros((COL, WIDE), F32), jnp.zeros((COL, WIDE), F32)
            acc_s = acc_n = None
            for h in range(HEADS):
                z = scores[h * WIN : (h + 1) * WIN]
                if i == 0:
                    z = jnp.concatenate(
                        [jnp.where(late, edge[h * COL : (h + 1) * COL], z[:COL]), z[COL:]], axis=0)
                z = z + bias[w, h].reshape(WIN, WIN)
                hm = value_mask(h)
                p = weights_of(z)
                ts, tn = mm(p, vs * hm), mm(p, vn * hm)
                acc_s = ts if acc_s is None else acc_s + ts
                acc_n = tn if acc_n is None else acc_n + tn
                if i == 0:
                    p2 = p.astype(F32)[:COL].astype(BF)
                    fix_s = fix_s + mm(p2, vs2 * hm)
                    fix_n = fix_n + mm(p2, vn2 * hm)
            tall = lambda a: a.reshape(-1, RPS, TILE, WIDE)
            acc = jnp.where(lower, tall(acc_s), tall(acc_n))
            if i == 0:
                fix = jnp.where(
                    lower, tall(fix_s), tall(fix_n))
                acc = jnp.concatenate([jnp.where(cell == 0, acc[:1], fix), acc[1:]], axis=0)
            att = mm(divide(acc.reshape(WIN, WIDE)), wproj[1])
            sl = slice(i * PAIRS, (i + 1) * PAIRS)
            r_s[w, sl] = f1[w, sl] + tiles(att)
        r_s[w] = ffn(1, r_s[w].reshape(-1, C), up, down).reshape(own, RPS, TILE, C)
    low = (iota((TILE, 1), 0) & 3) < 2
    cell, level = cell[0, 0], level[0, 0]
    for k in range(own):
        nxt = (k + 1) % own
        for rp in range(RPS):
            n0, n1 = (jnp.where(cell == 0, r_s[w, k, rp], r_s[w, nxt, rp]) for w in range(2))
            t0, t1 = jnp.where(level == 1, n0, n1), jnp.where(level == 0, n0, n1)
            a = jnp.where(low, t0, pltpu.roll(t1, 2, 0))
            b = jnp.where(low, pltpu.roll(t0, 6, 0), t1)
            pair = jnp.concatenate([a, b], axis=1)
            for d in range(2):
                out[2 * rp + d, :, 2 * k * C : 2 * (k + 1) * C] = pair[4 * d : 4 * d + 4].astype(BF)


def call(kernel, scalars, args, outs, scratch, name):
    return pl.pallas_call(
        kernel,
        out_shape=outs,
        in_specs=[SM] * len(scalars) + [VM] * len(args),
        out_specs=[VM] * len(outs),
        scratch_shapes=scratch,
        compiler_params=pltpu.CompilerParams(vmem_limit_bytes=32 * 2**20),
        cost_estimate=pl.CostEstimate(
            flops=2 * 10**9, bytes_accessed=6 * 10**6, transcendentals=10**6
        ),
        name=name,
    )(*scalars, *args)


def shifted(x, axis, by):
    size = lax.axis_size(axis)
    return lax.ppermute(x, axis, [(i, (i + by) % size) for i in range(size)])


def body(field, shift, window_type, qkv_weight, proj_weight, up_weight, down_weight, bias_table):
    own = field.shape[2] // C // 2
    wide = own + PAIRS
    half = WLON * C
    x = field.transpose(1, 0, 2)
    weights = (qkv_weight, proj_weight, up_weight, down_weight.transpose(0, 2, 1))
    table = bias_table.transpose(0, 2, 1, 3)
    dev = jnp.stack([lax.axis_index("lat"), jnp.int32(lax.axis_size("lat"))]).astype(jnp.int32)
    east = shifted(x[:, :, :half], "lon", -1)
    west = shifted(x[:, :, x.shape[2] - half :], "lon", 1)
    bias0 = bias_call(0, window_type, shift, dev, table)
    sds = jax.ShapeDtypeStruct
    cps = own + 2 * PAIRS
    rows = 2 * wide * 20
    pay = (rows + split_point(rows), 128)
    f1, ext, pay_up, pay_dn = call(
        first_kernel, (), (x, east, west, bias0) + weights,
        [sds((2, own, RPS, TILE, C), F32), sds((2, wide, RPS, TILE, C), F32),
         sds(pay, BF), sds(pay, BF)],
        [pltpu.VMEM((2, cps, RPS, TILE, C), F32), pltpu.VMEM((2, wide + 1, RPS, TILE, C), F32)]
        + [pltpu.VMEM((2 * cps * COL, C), BF)] * 2 + [pltpu.VMEM((2 * cps * COL, WIDE), BF)],
        "block0")
    below = shifted(pay_up, "lat", -1)
    above = shifted(pay_dn, "lat", 1)
    bias1 = bias_call(1, window_type, shift, dev, table)
    (out,) = call(
        second_kernel, (shift,), (f1, ext, above, below, bias1) + weights,
        [sds(x.shape, BF)],
        [pltpu.VMEM((2 * wide * COL, n), BF) for n in (C, WIDE, C, WIDE)] + [pltpu.VMEM((2 * own * COL, C), BF)] * 2
        + [pltpu.VMEM((2, own, RPS, TILE, C), F32)],
        "block1")
    return out.transpose(1, 0, 2)


def solution(mesh):
    return jax.shard_map(
        body,
        mesh=mesh,
        in_specs=(P(None, "lat", "lon"), P(), P(), P(), P(), P(), P(), P()),
        out_specs=P(None, "lat", "lon"),
        check_vma=False,
    )
```

```python
import functools

import jax
import jax.numpy as jnp
from jax import lax
from jax.experimental import pallas as pl
from jax.experimental.pallas import tpu as pltpu
from jax.sharding import PartitionSpec as P


HEADS = 6
HEAD_DIM = 32
C = 192
FF = 768
WLAT = 6
WLON = 12
TILE = 8
PAIRS = WLON // 2
RPS = WLAT // 2
COL = RPS * TILE
WIN = PAIRS * COL
SPAN = WLAT * (2 * WLON - 1)
NEG = -1e30
LOG2E = 1.4426950408889634
TURN, LAT, TYPES = 0, 2, 4
F32 = jnp.float32
BF = jnp.bfloat16


def mm(a, b):
    return jnp.dot(a, b, preferred_element_type=F32)


def mm_nt(a, b):
    return lax.dot_general(a, b, (((1,), (1,)), ((), ())), preferred_element_type=F32)


def norm(x, short):
    ones = jnp.ones((C, C), BF)
    high = x.astype(BF)
    total = mm(high, ones)
    if not short:
        total = total + mm((x - high.astype(F32)).astype(BF), ones)
    center = x - total * (1.0 / C)
    spread = mm((center * center).astype(BF), ones) * (1.0 / C)
    return center * lax.rsqrt(spread + 1e-05)


def gelu(x):
    return 0.5 * x * (1.0 + lax.erf(x * 0.7071067811865476))


def iota(shape, dim):
    return lax.broadcasted_iota(jnp.int32, shape, dim)


def qk(q, k):
    n = q.shape[0]
    parts = []
    for lo, hi in ((0, 128), (128, C)):
        lane = iota((1, hi - lo), 1)
        stack = []
        for h in range((hi - lo) // HEAD_DIM):
            hit = (lane >= h * HEAD_DIM) & (lane < (h + 1) * HEAD_DIM)
            stack.append(q[:, lo:hi] * hit.astype(F32).astype(BF))
        res = mm_nt(jnp.concatenate(stack, axis=0), k[:, lo:hi])
        parts += [res[h * n : (h + 1) * n] for h in range(len(stack))]
    return parts


WIDE = 256


def value_mask(h):
    lane = iota((1, WIDE), 1)
    hit = (lane >= h * HEAD_DIM) & (lane < (h + 1) * HEAD_DIM) | (lane == C + h)
    if h == 0:
        hit = hit | (lane >= C + HEADS)
    return hit.astype(F32).astype(BF)


def divide(acc):
    tail = acc[:, 128:]
    inv = 1.0 / jnp.where(iota((1, 128), 1) >= 64, tail, 1.0)
    high = inv.astype(BF)
    low = (inv - high.astype(F32)).astype(BF)
    i, lane = iota((128, C), 0), iota((128, C), 1)
    first = (i - 64) * HEAD_DIM
    spread = ((lane >= first) & (lane < first + HEAD_DIM)).astype(F32).astype(BF)
    return (acc[:, :C] * (mm(high, spread) + mm(low, spread))).astype(BF)


def tile_bits(shape, dim):
    s = iota(shape, dim)
    return s >> 2, (s >> 1) & 1, s & 1


def build_bias(block, sc, tab, out_ref, cut):
    t = sc[TURN] if block else 0
    lat, lats = sc[LAT], sc[LAT + 1]
    for h in range(HEADS):
        rows = tab[block, h].astype(F32)
        for p1 in range(2):
            for p2 in range(2):
                for i1 in range(WLAT):
                    a = ((p1 * 2 + p2) * WLAT + i1) * SPAN
                    at = (p1 * WLAT + i1) * 16
                    cut[h, p2, at : at + 16, :] = rows[:, a : a + SPAN].astype(BF)
    n, src = 2 * COL, 2 * WLAT * 16
    o, s = iota((n, src), 0), iota((n, src), 1)
    lw = (o >= COL).astype(jnp.int32)
    q = o - COL * lw
    r1 = 2 * (q >> 3) + ((q >> 2) & 1)
    p1 = (q & 1) ^ block
    own = r1 >= t
    i1 = jnp.where(own, r1 - t, r1 - t + WLAT)
    north = lax.rem(lat + lats - 1, lats)
    kind = jnp.where(
        lw == 0,
        jnp.where(own, sc[TYPES + lat], sc[TYPES + north]),
        jnp.where(own, sc[TYPES + lats + lat], sc[TYPES + lats + north]),
    )
    hit = s == (p1 * WLAT + i1) * 16 + kind
    cell = (q >> 1) & 1
    picks = [(hit & (cell == b)).astype(F32).astype(BF) for b in range(2)]
    pick2 = jnp.concatenate(picks, axis=0)
    left = [[[], []], [[], []]]
    for p2 in range(2):
        for h in range(HEADS):
            both = mm(pick2, cut[h, p2]).astype(BF)
            for b in range(2):
                left[b][p2].append(both[b * n : (b + 1) * n])
    left = [[jnp.concatenate(x, axis=0) for x in y] for y in left]
    m = iota((1, WIN), 1)
    cp2 = (m * 171) >> 12
    u = m - cp2 * COL
    r2 = 2 * (u >> 3) + ((u >> 2) & 1)
    j2 = 2 * cp2 + (((u >> 1) & 1) ^ block)
    p2m = (u & 1) ^ block
    i2 = jnp.where(r2 >= t, r2 - t, r2 - t + WLAT)
    place = i2 * (2 * WLON - 1) + (WLON - 1) - j2
    k = iota((SPAN, WIN), 0)
    mask = None
    if block:
        o = iota((n, WIN), 0)
        lw = (o >= COL).astype(jnp.int32)
        q = o - COL * lw
        r1 = 2 * (q >> 3) + ((q >> 2) & 1)
        south = r1 >= t
        edge = (south & (lat == lats - 1)) | (~south & (lat == 0))
        dead = (lw == 1) & (((q & 1) ^ block) != p2m)
        dead = dead | (edge & ((r1 < t) != (r2 < t)))
        mask = jnp.where(dead, NEG, 0.0).astype(F32)
        mask = jnp.concatenate([mask] * HEADS, axis=0)
    for cp1 in range(PAIRS):
        acc = None
        for b in range(2):
            j1 = 2 * cp1 + (b ^ block)
            for p2 in range(2):
                target = jnp.where(p2m == p2, place + j1, -1)
                pick = (k == target).astype(F32).astype(BF)
                term = mm(left[b][p2], pick)
                acc = term if acc is None else acc + term
        acc = acc * LOG2E
        if block:
            acc = acc + mask
        for h in range(HEADS):
            for lw in range(2):
                out_ref[lw, h, cp1] = acc[(2 * h + lw) * COL : (2 * h + lw + 1) * COL]


VM = pl.BlockSpec(memory_space=pltpu.VMEM)
SM = pl.BlockSpec(memory_space=pltpu.SMEM)


BIAS_SHAPE = (2, HEADS, PAIRS, COL, WIN)
CUT_SHAPE = (HEADS, 2, 2 * WLAT * 16, SPAN)


def ffn(block, mid, up, down):
    h_in = norm(mid, False).astype(BF)
    out = mid
    for f in range(0, FF, 256):
        hid = gelu(mm(h_in, up[block, :, f : f + 256])).astype(BF)
        out = out + mm_nt(hid, down[block, :, f : f + 256])
    return out.astype(BF).astype(F32)


def weights_of(z):
    return jnp.exp2(z - jnp.max(z, axis=-1, keepdims=True)).astype(BF)


def split_point(rows):
    return (rows // 2 + 15) // 16 * 16


def fold(y):
    rows = y.shape[0]
    half = split_point(rows)
    tail = jnp.concatenate([y[half:, 128:], jnp.zeros((2 * half - rows, 64), F32)], axis=0)
    high = jnp.concatenate([y[:half, 128:], tail], axis=1)
    return jnp.concatenate([y[:, :128], high], axis=0).astype(BF)


def unfold(data, rows):
    half = data.shape[0] - rows
    data = data.astype(F32)
    high = jnp.concatenate([data[rows:, :64], data[rows : 2 * rows - half, 64:]], axis=0)
    return jnp.concatenate([data[:rows], high], axis=1)


def tiles_of(ref, rp, k):
    two = jnp.concatenate(
        [ref[2 * rp + d, :, 2 * k * C : 2 * (k + 1) * C].astype(F32) for d in range(2)], axis=0
    )
    a, b = two[:, :C], two[:, C:]
    low = (iota((TILE, 1), 0) & 3) < 2
    return jnp.where(low, a, pltpu.roll(b, 2, 0)), jnp.where(low, pltpu.roll(a, 6, 0), b)


def project(x, w, block, at):
    return mm(x, w[block, :, at * C : (at + 1) * C])


def attend0(wins, bias, wqkv, wproj, up, down, x_s, q_s, k_s, v_s, acc_s):
    n = x_s.shape[1] * COL
    v_s[:, C:] = jnp.ones((2 * n, WIDE - C), BF)
    outs = []
    for lw in range(2):
        at = slice(lw * n, (lw + 1) * n)
        xn = norm(x_s[lw].reshape(n, C), True).astype(BF)
        q_s[at, :] = (project(xn, wqkv, 0, 0) * (HEAD_DIM**-0.5 * LOG2E)).astype(BF)
        k_s[at, :] = project(xn, wqkv, 0, 1).astype(BF)
        v_s[at, :C] = project(xn, wqkv, 0, 2).astype(BF)
    for lw in range(2):
        done, base = 0, []
        for first, skip in wins:
            at = lw * n + first * COL
            rows = WIN - skip * COL
            q = q_s[at : at + WIN, :]
            if skip:
                q = q.astype(F32)[skip * COL :].astype(BF)
            scores = qk(q, k_s[at : at + WIN, :])
            v = v_s[at : at + WIN, :]
            acc = None
            for h in range(HEADS):
                z = scores[h] + bias[lw, h, skip:].reshape(rows, WIN)
                term = mm(weights_of(z), v * value_mask(h))
                acc = term if acc is None else acc + term
            acc_s[done : done + rows, :] = acc
            done += rows
            base.append(x_s[lw, first + skip : first + PAIRS].reshape(rows, C))
        att = mm(divide(acc_s[:done, :]), wproj[0])
        outs.append(ffn(0, jnp.concatenate(base, axis=0) + att, up, down))
    return outs


def own_kernel(
    x, bias, wqkv, wproj, up, down, f_ref, n_ref, x_s, q_s, k_s, v_s, acc_s,
):
    cps = x_s.shape[1]
    for cp in range(cps):
        for rp in range(RPS):
            x_s[0, cp, rp], x_s[1, cp, rp] = tiles_of(x, rp, cp)
    wins = [(i, 0) for i in range(0, cps, PAIRS)]
    outs = attend0(wins, bias, wqkv, wproj, up, down, x_s, q_s, k_s, v_s, acc_s)
    for lw in range(2):
        f_ref[lw] = outs[lw].reshape(cps, RPS, TILE, C)
        n_ref[lw] = norm(outs[lw], True).reshape(cps, RPS, TILE, C)


def edge_kernel(
    east, west, bias, f_own, n_own, wqkv, wproj, up, down,
    f_ref, ext_ref, up_ref, dn_ref, x_s, q_s, k_s, v_s, acc_s,
):
    for cp in range(2 * PAIRS):
        ref, k = (east, cp) if cp < PAIRS else (west, cp - PAIRS)
        for rp in range(RPS):
            x_s[0, cp, rp], x_s[1, cp, rp] = tiles_of(ref, rp, k)
    wins = [(0, 0), (PAIRS, PAIRS - 1)]
    outs = attend0(wins, bias, wqkv, wproj, up, down, x_s, q_s, k_s, v_s, acc_s)
    side = [norm(o, True).reshape(-1, RPS, TILE, C) for o in outs]
    own = f_own.shape[1]
    _, cell, level = tile_bits((1, 1, TILE, 1), 2)
    keep = [level == 1, level == 0]
    for w in range(2):
        pick = lambda a: jnp.where(keep[w], a[0], a[1])
        mine = pick(f_own)
        before = jnp.concatenate([mine[own - 1 :], mine[: own - 1]], axis=0)
        f_ref[w] = jnp.where(cell == 0, mine, before)
        beside = pick(side)
        o = jnp.concatenate([beside[PAIRS:], pick(n_own), beside[:PAIRS]], axis=0)
        ext_ref[w] = jnp.where(cell == 0, o[1:], o[:-1])
    e = [ext_ref[w] for w in range(2)]
    top = (iota((1, TILE, 1), 1)) < 4
    flat = lambda a: a.reshape(-1, C)
    roll4 = lambda a: pltpu.roll(a, 4, 1)
    half = jnp.where(top, e[0][:, 2], roll4(e[1][:, 2]))
    up_ref[...] = fold(jnp.concatenate([flat(e[0][:, :2]), flat(e[1][:, :2]), flat(half)], axis=0))
    half = jnp.where(top, roll4(e[1][:, 0]), e[0][:, 0])
    dn_ref[...] = fold(jnp.concatenate([flat(e[0][:, 1:]), flat(e[1][:, 1:]), flat(half)], axis=0))


def row_of_tile():
    shape = (1, RPS, TILE, 1)
    return 2 * iota(shape, 1) + tile_bits(shape, 2)[0]


def tiles(a):
    return a.reshape(-1, RPS, TILE, a.shape[-1])


def ready_kernel(sc, tab, ext, wqkv, bias, k_ref, v_ref, qs_ref, qn_ref, cut):
    own = qs_ref.shape[0] // 2 // COL
    n = ext.shape[1] * COL
    lower = row_of_tile() >= sc[TURN]
    cell = tile_bits((1, 1, TILE, 1), 2)[1]
    for w in range(2):
        x = ext[w].reshape(n, C).astype(BF)
        k_ref[w * n : (w + 1) * n, :] = project(x, wqkv, 1, 1)
        v_ref[w * n : (w + 1) * n, :] = project(x, wqkv, 1, 2)
        fix = jnp.where(cell == 0, ext[w, :1], ext[w, own : own + 1])
        x = jnp.concatenate([fix, ext[w, 1:own]], axis=0).reshape(-1, C).astype(BF)
        q = tiles(project(x, wqkv, 1, 0) * (HEAD_DIM**-0.5 * LOG2E))
        at = slice(w * own * COL, (w + 1) * own * COL)
        qs_ref[at, :] = jnp.where(lower, q, 0.0).reshape(-1, C).astype(BF)
        qn_ref[at, :] = jnp.where(lower, 0.0, q).reshape(-1, C).astype(BF)
    build_bias(1, sc, tab, bias, cut)


def second_kernel(
    sc, f1, above, below, bias, k_own, v_own, qs_ref, qn_ref, wqkv, wproj, up, down,
    out, ks_s, vs_s, kn_s, vn_s, r_s, acc_s,
):
    t = sc[TURN]
    own = f1.shape[1]
    n = k_own.shape[0] // 2
    wide = n // COL
    south = unfold(below[...], 2 * wide * 20)
    north = unfold(above[...], 2 * wide * 20)
    full = wide * 16
    roll4 = lambda a: pltpu.roll(a, 4, 1)

    def halves(y):
        rest = y[2 * full :].reshape(wide, TILE, C)
        return [y[w * full : (w + 1) * full].reshape(wide, 2, TILE, C) for w in range(2)], rest

    (s_full, s_half), (n_full, n_half) = halves(south), halves(north)
    lower = row_of_tile() >= t
    cell = tile_bits((1, 1, TILE, 1), 2)[1]
    for w in range(2):
        low = jnp.concatenate(
            [s_full[w], (roll4(s_half) if w else s_half)[:, None]], axis=1)
        high = jnp.concatenate(
            [(roll4(n_half) if w else n_half)[:, None], n_full[w]], axis=1)
        x = jnp.where(lower, high, low).reshape(n, C).astype(BF)
        at = slice(w * n, (w + 1) * n)
        mine, other = tiles(k_own[at, :]), tiles(project(x, wqkv, 1, 1))
        ks_s[at, :] = jnp.where(lower, mine, other).reshape(n, C).astype(BF)
        kn_s[at, :] = jnp.where(lower, other, mine).reshape(n, C).astype(BF)
        mine, other = tiles(v_own[at, :]), tiles(project(x, wqkv, 1, 2))
        vs_s[at, :C] = jnp.where(lower, mine, other).reshape(n, C).astype(BF)
        vn_s[at, :C] = jnp.where(lower, other, mine).reshape(n, C).astype(BF)
    vs_s[:, C:] = vn_s[:, C:] = jnp.ones((2 * n, WIDE - C), BF)
    late = ((iota((COL, 1), 0) >> 1) & 1) == 1
    last = own // PAIRS
    for w in range(2):
        for i in range(own // PAIRS):
            at = slice(w * own * COL + i * WIN, w * own * COL + (i + 1) * WIN)
            qs, qn = qs_ref[at, :], qn_ref[at, :]
            pick = lambda ref, j: ref[w * n + j * WIN : w * n + (j + 1) * WIN, :]
            scores = [
                a + b for a, b in zip(qk(qs, pick(ks_s, i)), qk(qn, pick(kn_s, i)))]
            vs, vn = pick(vs_s, i), pick(vn_s, i)
            if i == 0:
                first = lambda q: q.astype(F32)[:COL].astype(BF)
                edge = [
                    a + b
                    for a, b in zip(
                        qk(first(qs), pick(ks_s, last)), qk(first(qn), pick(kn_s, last)))]
                vs2, vn2 = pick(vs_s, last), pick(vn_s, last)
                fix_s, fix_n = jnp.zeros((COL, WIDE), F32), jnp.zeros((COL, WIDE), F32)
            sum_s = sum_n = None
            for h in range(HEADS):
                z = scores[h]
                if i == 0:
                    z = jnp.concatenate([jnp.where(late, edge[h], z[:COL]), z[COL:]], axis=0)
                p = weights_of(z + bias[w, h].reshape(WIN, WIN))
                hm = value_mask(h)
                ts, tn = mm(p, vs * hm), mm(p, vn * hm)
                sum_s = ts if sum_s is None else sum_s + ts
                sum_n = tn if sum_n is None else sum_n + tn
                if i == 0:
                    p2 = p.astype(F32)[:COL].astype(BF)
                    fix_s = fix_s + mm(p2, vs2 * hm)
                    fix_n = fix_n + mm(p2, vn2 * hm)
            acc = jnp.where(lower, tiles(sum_s), tiles(sum_n))
            if i == 0:
                fix = jnp.where(lower, tiles(fix_s), tiles(fix_n))
                acc = jnp.concatenate([jnp.where(cell == 0, acc[:1], fix), acc[1:]], axis=0)
            acc_s[i * WIN : (i + 1) * WIN, :] = acc.reshape(WIN, WIDE)
        att = mm(divide(acc_s[...]), wproj[1])
        r_s[w] = tiles(ffn(1, f1[w].reshape(-1, C) + att, up, down))
    low = (iota((TILE, 1), 0) & 3) < 2
    _, cell, level = tile_bits((TILE, 1), 0)
    for k in range(own):
        nxt = (k + 1) % own
        for rp in range(RPS):
            n0, n1 = (jnp.where(cell == 0, r_s[w, k, rp], r_s[w, nxt, rp]) for w in range(2))
            t0, t1 = jnp.where(level == 1, n0, n1), jnp.where(level == 0, n0, n1)
            a = jnp.where(low, t0, pltpu.roll(t1, 2, 0))
            b = jnp.where(low, pltpu.roll(t0, 6, 0), t1)
            pair = jnp.concatenate([a, b], axis=1)
            for d in range(2):
                out[2 * rp + d, :, 2 * k * C : 2 * (k + 1) * C] = pair[4 * d : 4 * d + 4].astype(BF)


VM = pl.BlockSpec(memory_space=pltpu.VMEM)
SM = pl.BlockSpec(memory_space=pltpu.SMEM)


def call(kernel, scalars, args, outs, scratch, name, flops):
    return pl.pallas_call(
        kernel,
        out_shape=outs,
        in_specs=[SM] * len(scalars) + [VM] * len(args),
        out_specs=[VM] * len(outs),
        scratch_shapes=scratch,
        compiler_params=pltpu.CompilerParams(vmem_limit_bytes=24 * 2**20),
        cost_estimate=pl.CostEstimate(
            flops=flops, bytes_accessed=4 * 10**6, transcendentals=10**6
        ),
        name=name,
    )(*scalars, *args)


def shifted(x, axis, by):
    size = lax.axis_size(axis)
    return lax.ppermute(x, axis, [(i, (i + by) % size) for i in range(size)])


def body(field, shift, window_type, qkv_weight, proj_weight, up_weight, down_weight, bias_table):
    own = field.shape[2] // C // 2
    wide = own + PAIRS
    half = WLON * C
    x = field.transpose(1, 0, 2)
    weights = (qkv_weight, proj_weight, up_weight, down_weight.transpose(0, 2, 1))
    table = bias_table.transpose(0, 2, 1, 3)
    dev = jnp.stack([lax.axis_index("lat"), jnp.int32(lax.axis_size("lat"))]).astype(jnp.int32)
    scalars = jnp.concatenate([shift, dev, window_type.reshape(-1)])
    east = shifted(x[:, :, :half], "lon", -1)
    west = shifted(x[:, :, x.shape[2] - half :], "lon", 1)
    sds = jax.ShapeDtypeStruct
    rows = 2 * wide * 20
    pay = (rows + split_point(rows), 128)
    tile = lambda cps: (2, cps, RPS, TILE, C)
    cut = pltpu.VMEM(CUT_SHAPE, BF)

    def scratch(cps, rows):
        n = 2 * cps * COL
        return [pltpu.VMEM(tile(cps), F32), pltpu.VMEM((n, C), BF), pltpu.VMEM((n, C), BF),
                pltpu.VMEM((n, WIDE), BF), pltpu.VMEM((rows, WIDE), F32)]

    (bias0,) = call(
        functools.partial(build_bias, 0), (scalars,), (table,), [sds(BIAS_SHAPE, F32)], [cut],
        "bias0", 10**9)
    f_own, n_own = call(
        own_kernel, (), (x, bias0) + weights, [sds(tile(own), F32), sds(tile(own), F32)],
        scratch(own, own * COL), "own0", 2 * 10**9)
    f1, ext, pay_up, pay_dn = call(
        edge_kernel, (), (east, west, bias0, f_own, n_own) + weights,
        [sds(tile(own), F32), sds(tile(wide), F32), sds(pay, BF), sds(pay, BF)],
        scratch(2 * PAIRS, WIN + COL), "edge0", 2 * 10**9)
    below = shifted(pay_up, "lat", -1)
    above = shifted(pay_dn, "lat", 1)
    m, n = 2 * wide * COL, 2 * own * COL
    bias1, k_own, v_own, qs, qn = call(
        ready_kernel, (scalars,), (table, ext, qkv_weight),
        [sds(BIAS_SHAPE, F32), sds((m, C), F32), sds((m, C), F32), sds((n, C), BF), sds((n, C), BF)],
        [cut], "ready1", 2 * 10**9)
    (out,) = call(
        second_kernel, (scalars,), (f1, above, below, bias1, k_own, v_own, qs, qn) + weights,
        [sds(x.shape, BF)],
        [pltpu.VMEM((m, lanes), BF) for lanes in (C, WIDE, C, WIDE)]
        + [pltpu.VMEM(tile(own), F32), pltpu.VMEM((own * COL, WIDE), F32)],
        "block1", 2 * 10**9)
    return out.transpose(1, 0, 2)


def solution(mesh):
    return jax.shard_map(
        body,
        mesh=mesh,
        in_specs=(P(None, "lat", "lon"), P(), P(), P(), P(), P(), P(), P()),
        out_specs=P(None, "lat", "lon"),
        check_vma=False,
    )
```

```python
import functools

import jax
import jax.numpy as jnp
from jax import lax
from jax.experimental import pallas as pl
from jax.experimental.pallas import tpu as pltpu
from jax.sharding import PartitionSpec as P


HEADS = 6
HEAD_DIM = 32
C = 192
FF = 768
WLAT = 6
WLON = 12
TILE = 8
PAIRS = WLON // 2
RPS = WLAT // 2
COL = RPS * TILE
WIN = PAIRS * COL
SPAN = WLAT * (2 * WLON - 1)
NEG = -1e30
LOG2E = 1.4426950408889634
F32 = jnp.float32
BF = jnp.bfloat16


def mm(a, b):
    return jnp.dot(a, b, preferred_element_type=F32)


def mm_nt(a, b):
    return lax.dot_general(a, b, (((1,), (1,)), ((), ())), preferred_element_type=F32)


def norm(x, short):
    ones = jnp.ones((C, C), BF)
    high = x.astype(BF)
    total = mm(high, ones)
    if not short:
        total = total + mm((x - high.astype(F32)).astype(BF), ones)
    center = x - total * (1.0 / C)
    spread = mm((center * center).astype(BF), ones) * (1.0 / C)
    return center * lax.rsqrt(spread + 1e-05)


def gelu(x):
    return 0.5 * x * (1.0 + lax.erf(x * 0.7071067811865476))


def iota(shape, dim):
    return lax.broadcasted_iota(jnp.int32, shape, dim)


def qk(q, k):
    n = q.shape[0]
    parts = []
    for lo, hi in ((0, 128), (128, C)):
        lane = iota((1, hi - lo), 1)
        stack = []
        for h in range((hi - lo) // HEAD_DIM):
            hit = (lane >= h * HEAD_DIM) & (lane < (h + 1) * HEAD_DIM)
            stack.append(q[:, lo:hi] * hit.astype(F32).astype(BF))
        res = mm_nt(jnp.concatenate(stack, axis=0), k[:, lo:hi])
        parts += [res[h * n : (h + 1) * n] for h in range(len(stack))]
    return parts


WIDE = 256


def value_mask(h):
    lane = iota((1, WIDE), 1)
    hit = (lane >= h * HEAD_DIM) & (lane < (h + 1) * HEAD_DIM) | (lane == C + h)
    if h == 0:
        hit = hit | (lane >= C + HEADS)
    return hit.astype(F32).astype(BF)


def divide(acc):
    tail = acc[:, 128:]
    inv = 1.0 / jnp.where(iota((1, 128), 1) >= 64, tail, 1.0)
    high = inv.astype(BF)
    low = (inv - high.astype(F32)).astype(BF)
    i, lane = iota((128, C), 0), iota((128, C), 1)
    first = (i - 64) * HEAD_DIM
    spread = ((lane >= first) & (lane < first + HEAD_DIM)).astype(F32).astype(BF)
    return (acc[:, :C] * (mm(high, spread) + mm(low, spread))).astype(BF)


def tile_bits(shape, dim):
    s = iota(shape, dim)
    return s >> 2, (s >> 1) & 1, s & 1


def build_bias(block, t, sc, tab, out_ref, cut):
    lat, lats = sc[2, 0], sc.shape[1]
    for h in range(HEADS):
        rows = tab[block, h].astype(F32)
        for p1 in range(2):
            for p2 in range(2):
                for i1 in range(WLAT):
                    a = ((p1 * 2 + p2) * WLAT + i1) * SPAN
                    at = (p1 * WLAT + i1) * 16
                    cut[h, p2, at : at + 16, :] = rows[:, a : a + SPAN].astype(BF)
    n, src = 2 * COL, 2 * WLAT * 16
    o, s = iota((n, src), 0), iota((n, src), 1)
    lw = (o >= COL).astype(jnp.int32)
    q = o - COL * lw
    r1 = 2 * (q >> 3) + ((q >> 2) & 1)
    p1 = (q & 1) ^ block
    own = r1 >= t
    i1 = jnp.where(own, r1 - t, r1 - t + WLAT)
    north = lax.rem(lat + lats - 1, lats)
    kind = jnp.where(
        lw == 0,
        jnp.where(own, sc[0, lat], sc[0, north]),
        jnp.where(own, sc[1, lat], sc[1, north]),
    )
    hit = s == (p1 * WLAT + i1) * 16 + kind
    cell = (q >> 1) & 1
    picks = [(hit & (cell == b)).astype(F32).astype(BF) for b in range(2)]
    pick2 = jnp.concatenate(picks, axis=0)
    left = [[[], []], [[], []]]
    for p2 in range(2):
        for h in range(HEADS):
            both = mm(pick2, cut[h, p2]).astype(BF)
            for b in range(2):
                left[b][p2].append(both[b * n : (b + 1) * n])
    left = [[jnp.concatenate(x, axis=0) for x in y] for y in left]
    m = iota((1, WIN), 1)
    cp2 = (m * 171) >> 12
    u = m - cp2 * COL
    r2 = 2 * (u >> 3) + ((u >> 2) & 1)
    j2 = 2 * cp2 + (((u >> 1) & 1) ^ block)
    p2m = (u & 1) ^ block
    i2 = jnp.where(r2 >= t, r2 - t, r2 - t + WLAT)
    place = i2 * (2 * WLON - 1) + (WLON - 1) - j2
    k = iota((SPAN, WIN), 0)
    mask = None
    if block:
        o = iota((n, WIN), 0)
        lw = (o >= COL).astype(jnp.int32)
        q = o - COL * lw
        r1 = 2 * (q >> 3) + ((q >> 2) & 1)
        south = r1 >= t
        edge = (south & (lat == lats - 1)) | (~south & (lat == 0))
        dead = (lw == 1) & (((q & 1) ^ block) != p2m)
        dead = dead | (edge & ((r1 < t) != (r2 < t)))
        mask = jnp.where(dead, NEG, 0.0).astype(F32)
        mask = jnp.concatenate([mask] * HEADS, axis=0)
    for cp1 in range(PAIRS):
        acc = None
        for b in range(2):
            j1 = 2 * cp1 + (b ^ block)
            for p2 in range(2):
                target = jnp.where(p2m == p2, place + j1, -1)
                pick = (k == target).astype(F32).astype(BF)
                term = mm(left[b][p2], pick)
                acc = term if acc is None else acc + term
        acc = acc * LOG2E
        if block:
            acc = acc + mask
        for h in range(HEADS):
            for lw in range(2):
                out_ref[lw, h, cp1] = acc[(2 * h + lw) * COL : (2 * h + lw + 1) * COL]


VM = pl.BlockSpec(memory_space=pltpu.VMEM)
SM = pl.BlockSpec(memory_space=pltpu.SMEM)


BIAS_SHAPE = (2, HEADS, PAIRS, COL, WIN)
CUT_SHAPE = (HEADS, 2, 2 * WLAT * 16, SPAN)


def ffn(block, mid, up, down):
    h_in = norm(mid, False).astype(BF)
    out = mid
    for f in range(0, FF, 256):
        hid = gelu(mm(h_in, up[block, :, f : f + 256])).astype(BF)
        out = out + mm_nt(hid, down[block, :, f : f + 256])
    return out.astype(BF).astype(F32)


def weights_of(z):
    return jnp.exp2(z - jnp.max(z, axis=-1, keepdims=True)).astype(BF)


def split_point(rows):
    return (rows // 2 + 15) // 16 * 16


def fold(y):
    rows = y.shape[0]
    half = split_point(rows)
    tail = jnp.concatenate([y[half:, 128:], jnp.zeros((2 * half - rows, 64), F32)], axis=0)
    high = jnp.concatenate([y[:half, 128:], tail], axis=1)
    return jnp.concatenate([y[:, :128], high], axis=0).astype(BF)


def unfold(data, rows):
    half = data.shape[0] - rows
    high = jnp.concatenate([data[rows:, :64], data[rows : 2 * rows - half, 64:]], axis=0)
    return jnp.concatenate([data[:rows], high], axis=1)


def tiles_of(ref, rp, k):
    two = jnp.concatenate(
        [ref[2 * rp + d, :, 2 * k * C : 2 * (k + 1) * C].astype(F32) for d in range(2)], axis=0
    )
    a, b = two[:, :C], two[:, C:]
    low = (iota((TILE, 1), 0) & 3) < 2
    return jnp.where(low, a, pltpu.roll(b, 2, 0)), jnp.where(low, pltpu.roll(a, 6, 0), b)


def project(x, w, block, at):
    return mm(x, w[block, :, at * C : (at + 1) * C])


def attend0(wins, bias, wqkv, wproj, up, down, x_s, q_s, k_s, v_s, acc_s):
    n = x_s.shape[1] * COL
    v_s[:, C:] = jnp.ones((2 * n, WIDE - C), BF)
    outs = []
    for lw in range(2):
        at = slice(lw * n, (lw + 1) * n)
        xn = norm(x_s[lw].reshape(n, C), True).astype(BF)
        q_s[at, :] = (project(xn, wqkv, 0, 0) * (HEAD_DIM**-0.5 * LOG2E)).astype(BF)
        k_s[at, :] = project(xn, wqkv, 0, 1).astype(BF)
        v_s[at, :C] = project(xn, wqkv, 0, 2).astype(BF)
    for lw in range(2):
        done, base = 0, []
        for first, skip in wins:
            at = lw * n + first * COL
            rows = WIN - skip * COL
            q = q_s[at : at + WIN, :]
            if skip:
                q = q.astype(F32)[skip * COL :].astype(BF)
            scores = qk(q, k_s[at : at + WIN, :])
            v = v_s[at : at + WIN, :]
            acc = None
            for h in range(HEADS):
                z = scores[h] + bias[lw, h, skip:].reshape(rows, WIN)
                term = mm(weights_of(z), v * value_mask(h))
                acc = term if acc is None else acc + term
            acc_s[done : done + rows, :] = acc
            done += rows
            base.append(x_s[lw, first + skip : first + PAIRS].reshape(rows, C))
        att = mm(divide(acc_s[:done, :]), wproj[0])
        outs.append(ffn(0, jnp.concatenate(base, axis=0) + att, up, down))
    return outs


def own_kernel(
    x, bias, wqkv, wproj, up, down, f_ref, n_ref, x_s, q_s, k_s, v_s, acc_s,
):
    cps = x_s.shape[1]
    for cp in range(cps):
        for rp in range(RPS):
            x_s[0, cp, rp], x_s[1, cp, rp] = tiles_of(x, rp, cp)
    wins = [(i, 0) for i in range(0, cps, PAIRS)]
    outs = attend0(wins, bias, wqkv, wproj, up, down, x_s, q_s, k_s, v_s, acc_s)
    for lw in range(2):
        f_ref[lw] = outs[lw].reshape(cps, RPS, TILE, C)
        n_ref[lw] = norm(outs[lw], True).reshape(cps, RPS, TILE, C)


def edge_kernel(
    east, west, bias, n_own, wqkv, wproj, up, down,
    ext_ref, up_ref, dn_ref, x_s, q_s, k_s, v_s, acc_s,
):
    own = n_own.shape[1]
    for cp in range(2 * PAIRS):
        ref, k = (east, cp) if cp < PAIRS else (west, own - 2 * PAIRS + cp)
        for rp in range(RPS):
            x_s[0, cp, rp], x_s[1, cp, rp] = tiles_of(ref, rp, k)
    wins = [(0, 0), (PAIRS, PAIRS - 1)]
    outs = attend0(wins, bias, wqkv, wproj, up, down, x_s, q_s, k_s, v_s, acc_s)
    side = [norm(o, True).reshape(-1, RPS, TILE, C) for o in outs]
    _, cell, level = tile_bits((1, 1, TILE, 1), 2)
    keep = [level == 1, level == 0]
    for w in range(2):
        pick = lambda a: jnp.where(keep[w], a[0], a[1])
        beside = pick(side)
        o = jnp.concatenate([beside[PAIRS:], pick(n_own), beside[:PAIRS]], axis=0)
        ext_ref[w] = jnp.where(cell == 0, o[1:], o[:-1])
    e = [ext_ref[w] for w in range(2)]
    top = (iota((1, TILE, 1), 1)) < 4
    flat = lambda a: a.reshape(-1, C)
    roll4 = lambda a: pltpu.roll(a, 4, 1)
    half = jnp.where(top, e[0][:, 2], roll4(e[1][:, 2]))
    up_ref[...] = fold(jnp.concatenate([flat(e[0][:, :2]), flat(e[1][:, :2]), flat(half)], axis=0))
    half = jnp.where(top, roll4(e[1][:, 0]), e[0][:, 0])
    dn_ref[...] = fold(jnp.concatenate([flat(e[0][:, 1:]), flat(e[1][:, 1:]), flat(half)], axis=0))


def row_of_tile():
    shape = (1, RPS, TILE, 1)
    return 2 * iota(shape, 1) + tile_bits(shape, 2)[0]


def tiles(a):
    return a.reshape(-1, RPS, TILE, a.shape[-1])


def ready_kernel(sh, sc, tab, ext, f_own, wqkv, bias, f_ref, k_ref, v_ref, qs_ref, qn_ref, cut):
    own = qs_ref.shape[0] // 2 // COL
    n = ext.shape[1] * COL
    lower = row_of_tile() >= sh[0]
    _, cell, level = tile_bits((1, 1, TILE, 1), 2)
    for w in range(2):
        mine = jnp.where(level == 1 - w, f_own[0], f_own[1])
        before = jnp.concatenate([mine[own - 1 :], mine[: own - 1]], axis=0)
        f_ref[w] = jnp.where(cell == 0, mine, before)
        x = ext[w].reshape(n, C).astype(BF)
        k_ref[w * n : (w + 1) * n, :] = project(x, wqkv, 1, 1)
        v_ref[w * n : (w + 1) * n, :] = project(x, wqkv, 1, 2)
        fix = jnp.where(cell == 0, ext[w, :1], ext[w, own : own + 1])
        x = jnp.concatenate([fix, ext[w, 1:own]], axis=0).reshape(-1, C).astype(BF)
        q = tiles(project(x, wqkv, 1, 0) * (HEAD_DIM**-0.5 * LOG2E))
        at = slice(w * own * COL, (w + 1) * own * COL)
        qs_ref[at, :] = jnp.where(lower, q, 0.0).reshape(-1, C).astype(BF)
        qn_ref[at, :] = jnp.where(lower, 0.0, q).reshape(-1, C).astype(BF)
    build_bias(1, sh[0], sc, tab, bias, cut)


def second_kernel(
    sh, f1, above, below, bias, k_own, v_own, qs_ref, qn_ref, wqkv, wproj, up, down,
    out, ks_s, vs_s, kn_s, vn_s, r_s, acc_s,
):
    t = sh[0]
    own = f1.shape[1]
    n = k_own.shape[0] // 2
    wide = n // COL
    south = unfold(below[...].astype(F32), 2 * wide * 20)
    north = unfold(above[...].astype(F32), 2 * wide * 20)
    full = wide * 16
    roll4 = lambda a: pltpu.roll(a, 4, 1)

    def halves(y):
        rest = y[2 * full :].reshape(wide, TILE, C)
        return [y[w * full : (w + 1) * full].reshape(wide, 2, TILE, C) for w in range(2)], rest

    (s_full, s_half), (n_full, n_half) = halves(south), halves(north)
    lower = row_of_tile() >= t
    cell = tile_bits((1, 1, TILE, 1), 2)[1]
    for w in range(2):
        low = jnp.concatenate(
            [s_full[w], (roll4(s_half) if w else s_half)[:, None]], axis=1)
        high = jnp.concatenate(
            [(roll4(n_half) if w else n_half)[:, None], n_full[w]], axis=1)
        x = jnp.where(lower, high, low).reshape(n, C).astype(BF)
        at = slice(w * n, (w + 1) * n)
        mine, other = tiles(k_own[at, :]), tiles(project(x, wqkv, 1, 1))
        ks_s[at, :] = jnp.where(lower, mine, other).reshape(n, C).astype(BF)
        kn_s[at, :] = jnp.where(lower, other, mine).reshape(n, C).astype(BF)
        mine, other = tiles(v_own[at, :]), tiles(project(x, wqkv, 1, 2))
        vs_s[at, :C] = jnp.where(lower, mine, other).reshape(n, C).astype(BF)
        vn_s[at, :C] = jnp.where(lower, other, mine).reshape(n, C).astype(BF)
    vs_s[:, C:] = vn_s[:, C:] = jnp.ones((2 * n, WIDE - C), BF)
    late = ((iota((COL, 1), 0) >> 1) & 1) == 1
    last = own // PAIRS
    for w in range(2):
        for i in range(own // PAIRS):
            at = slice(w * own * COL + i * WIN, w * own * COL + (i + 1) * WIN)
            qs, qn = qs_ref[at, :], qn_ref[at, :]
            pick = lambda ref, j: ref[w * n + j * WIN : w * n + (j + 1) * WIN, :]
            scores = [
                a + b for a, b in zip(qk(qs, pick(ks_s, i)), qk(qn, pick(kn_s, i)))]
            vs, vn = pick(vs_s, i), pick(vn_s, i)
            if i == 0:
                first = lambda q: q.astype(F32)[:COL].astype(BF)
                edge = [
                    a + b
                    for a, b in zip(
                        qk(first(qs), pick(ks_s, last)), qk(first(qn), pick(kn_s, last)))]
                vs2, vn2 = pick(vs_s, last), pick(vn_s, last)
                fix_s, fix_n = jnp.zeros((COL, WIDE), F32), jnp.zeros((COL, WIDE), F32)
            sum_s = sum_n = None
            for h in range(HEADS):
                z = scores[h]
                if i == 0:
                    z = jnp.concatenate([jnp.where(late, edge[h], z[:COL]), z[COL:]], axis=0)
                p = weights_of(z + bias[w, h].reshape(WIN, WIN))
                hm = value_mask(h)
                ts, tn = mm(p, vs * hm), mm(p, vn * hm)
                sum_s = ts if sum_s is None else sum_s + ts
                sum_n = tn if sum_n is None else sum_n + tn
                if i == 0:
                    p2 = p.astype(F32)[:COL].astype(BF)
                    fix_s = fix_s + mm(p2, vs2 * hm)
                    fix_n = fix_n + mm(p2, vn2 * hm)
            acc = jnp.where(lower, tiles(sum_s), tiles(sum_n))
            if i == 0:
                fix = jnp.where(lower, tiles(fix_s), tiles(fix_n))
                acc = jnp.concatenate([jnp.where(cell == 0, acc[:1], fix), acc[1:]], axis=0)
            acc_s[i * WIN : (i + 1) * WIN, :] = acc.reshape(WIN, WIDE)
        att = mm(divide(acc_s[...]), wproj[1])
        r_s[w] = tiles(ffn(1, f1[w].reshape(-1, C) + att, up, down))
    low = (iota((TILE, 1), 0) & 3) < 2
    _, cell, level = tile_bits((TILE, 1), 0)
    for k in range(own):
        nxt = (k + 1) % own
        for rp in range(RPS):
            n0, n1 = (jnp.where(cell == 0, r_s[w, k, rp], r_s[w, nxt, rp]) for w in range(2))
            t0, t1 = jnp.where(level == 1, n0, n1), jnp.where(level == 0, n0, n1)
            a = jnp.where(low, t0, pltpu.roll(t1, 2, 0))
            b = jnp.where(low, pltpu.roll(t0, 6, 0), t1)
            pair = jnp.concatenate([a, b], axis=1)
            for d in range(2):
                out[2 * rp + d, :, 2 * k * C : 2 * (k + 1) * C] = pair[4 * d : 4 * d + 4].astype(BF)


VM = pl.BlockSpec(memory_space=pltpu.VMEM)
SM = pl.BlockSpec(memory_space=pltpu.SMEM)


def call(kernel, scalars, args, outs, scratch, name, flops):
    return pl.pallas_call(
        kernel,
        out_shape=outs,
        in_specs=[SM] * len(scalars) + [VM] * len(args),
        out_specs=[VM] * len(outs),
        scratch_shapes=scratch,
        compiler_params=pltpu.CompilerParams(vmem_limit_bytes=24 * 2**20),
        cost_estimate=pl.CostEstimate(
            flops=flops, bytes_accessed=4 * 10**6, transcendentals=10**6
        ),
        name=name,
    )(*scalars, *args)


def shifted(x, axis, by):
    size = lax.axis_size(axis)
    return lax.ppermute(x, axis, [(i, (i + by) % size) for i in range(size)])


def body(field, shift, window_type, qkv_weight, proj_weight, up_weight, down_weight, bias_table):
    own = field.shape[2] // C // 2
    wide = own + PAIRS
    x = field.transpose(1, 0, 2)
    weights = (qkv_weight, proj_weight, up_weight, down_weight.transpose(0, 2, 1))
    table = bias_table.transpose(0, 2, 1, 3)
    row = iota((3, window_type.shape[1]), 0)
    scalars = jnp.where(
        row == 2, lax.axis_index("lat"), jnp.pad(window_type, ((0, 1), (0, 0))))
    east = shifted(x, "lon", -1)
    west = shifted(x, "lon", 1)
    sds = jax.ShapeDtypeStruct
    rows = 2 * wide * 20
    pay = (rows + split_point(rows), 128)
    tile = lambda cps: (2, cps, RPS, TILE, C)
    cut = pltpu.VMEM(CUT_SHAPE, BF)

    def scratch(cps, rows):
        n = 2 * cps * COL
        return [pltpu.VMEM(tile(cps), F32), pltpu.VMEM((n, C), BF), pltpu.VMEM((n, C), BF),
                pltpu.VMEM((n, WIDE), BF), pltpu.VMEM((rows, WIDE), F32)]

    (bias0,) = call(
        functools.partial(build_bias, 0, 0), (scalars,), (table,), [sds(BIAS_SHAPE, F32)], [cut],
        "bias0", 10**9)
    f_own, n_own = call(
        own_kernel, (), (x, bias0) + weights, [sds(tile(own), F32), sds(tile(own), F32)],
        scratch(own, own * COL), "own0", 2 * 10**9)
    ext, pay_up, pay_dn = call(
        edge_kernel, (), (east, west, bias0, n_own) + weights,
        [sds(tile(wide), F32), sds(pay, BF), sds(pay, BF)],
        scratch(2 * PAIRS, WIN + COL), "edge0", 2 * 10**9)
    below = shifted(pay_up, "lat", -1)
    above = shifted(pay_dn, "lat", 1)
    m, n = 2 * wide * COL, 2 * own * COL
    bias1, f1, k_own, v_own, qs, qn = call(
        ready_kernel, (shift, scalars), (table, ext, f_own, qkv_weight),
        [sds(BIAS_SHAPE, F32), sds(tile(own), F32), sds((m, C), F32), sds((m, C), F32), sds((n, C), BF), sds((n, C), BF)],
        [cut], "ready1", 2 * 10**9)
    (out,) = call(
        second_kernel, (shift,), (f1, above, below, bias1, k_own, v_own, qs, qn) + weights,
        [sds(x.shape, BF)],
        [pltpu.VMEM((m, lanes), BF) for lanes in (C, WIDE, C, WIDE)]
        + [pltpu.VMEM(tile(own), F32), pltpu.VMEM((own * COL, WIDE), F32)],
        "block1", 2 * 10**9)
    return out.transpose(1, 0, 2)


def solution(mesh):
    return jax.shard_map(
        body,
        mesh=mesh,
        in_specs=(P(None, "lat", "lon"), P(), P(), P(), P(), P(), P(), P()),
        out_specs=P(None, "lat", "lon"),
        check_vma=False,
    )
```

```python
import functools

import jax
import jax.numpy as jnp
from jax import lax
from jax.experimental import pallas as pl
from jax.experimental.pallas import tpu as pltpu
from jax.sharding import PartitionSpec as P


HEADS = 6
HEAD_DIM = 32
C = 192
FF = 768
WLAT = 6
WLON = 12
TILE = 8
PAIRS = WLON // 2
RPS = WLAT // 2
COL = RPS * TILE
WIN = PAIRS * COL
SPAN = WLAT * (2 * WLON - 1)
NEG = -1e30
LOG2E = 1.4426950408889634
F32 = jnp.float32
BF = jnp.bfloat16


def mm(a, b):
    return jnp.dot(a, b, preferred_element_type=F32)


def mm_nt(a, b):
    return lax.dot_general(a, b, (((1,), (1,)), ((), ())), preferred_element_type=F32)


def norm(x):
    center = x - jnp.mean(x, axis=-1, keepdims=True)
    spread = mm((center * center).astype(BF), jnp.ones((C, C), BF)) * (1.0 / C)
    return center * lax.rsqrt(spread + 1e-05)


def gelu(x):
    return 0.5 * x * (1.0 + lax.erf(x * 0.7071067811865476))


def iota(shape, dim):
    return lax.broadcasted_iota(jnp.int32, shape, dim)


def qk(q, k):
    n = q.shape[0]
    parts = []
    for lo, hi in ((0, 128), (128, C)):
        lane = iota((1, hi - lo), 1)
        stack = []
        for h in range((hi - lo) // HEAD_DIM):
            hit = (lane >= h * HEAD_DIM) & (lane < (h + 1) * HEAD_DIM)
            stack.append(q[:, lo:hi] * hit.astype(F32).astype(BF))
        res = mm_nt(jnp.concatenate(stack, axis=0), k[:, lo:hi])
        parts += [res[h * n : (h + 1) * n] for h in range(len(stack))]
    return parts


WIDE = 256


def value_mask(h):
    lane = iota((1, WIDE), 1)
    hit = (lane >= h * HEAD_DIM) & (lane < (h + 1) * HEAD_DIM) | (lane == C + h)
    if h == 0:
        hit = hit | (lane >= C + HEADS)
    return hit.astype(F32).astype(BF)


def divide(acc):
    tail = acc[:, 128:]
    inv = 1.0 / jnp.where(iota((1, 128), 1) >= 64, tail, 1.0)
    high = inv.astype(BF)
    low = (inv - high.astype(F32)).astype(BF)
    i, lane = iota((128, C), 0), iota((128, C), 1)
    first = (i - 64) * HEAD_DIM
    spread = ((lane >= first) & (lane < first + HEAD_DIM)).astype(F32).astype(BF)
    return (acc[:, :C] * (mm(high, spread) + mm(low, spread))).astype(BF)


def tile_bits(shape, dim):
    s = iota(shape, dim)
    return s >> 2, (s >> 1) & 1, s & 1


def build_bias(block, t, sc, tab, out_ref, cut):
    lat, lats = sc[2, 0], sc.shape[1]
    for h in range(HEADS):
        rows = tab[block, h].astype(F32)
        for p1 in range(2):
            for p2 in range(2):
                for i1 in range(WLAT):
                    a = ((p1 * 2 + p2) * WLAT + i1) * SPAN
                    at = (p1 * WLAT + i1) * 16
                    cut[h, p2, at : at + 16, :] = rows[:, a : a + SPAN].astype(BF)
    n, src = 2 * COL, 2 * WLAT * 16
    o, s = iota((n, src), 0), iota((n, src), 1)
    lw = (o >= COL).astype(jnp.int32)
    q = o - COL * lw
    r1 = 2 * (q >> 3) + ((q >> 2) & 1)
    p1 = (q & 1) ^ block
    own = r1 >= t
    i1 = jnp.where(own, r1 - t, r1 - t + WLAT)
    north = lax.rem(lat + lats - 1, lats)
    kind = jnp.where(
        lw == 0,
        jnp.where(own, sc[0, lat], sc[0, north]),
        jnp.where(own, sc[1, lat], sc[1, north]),
    )
    hit = s == (p1 * WLAT + i1) * 16 + kind
    cell = (q >> 1) & 1
    picks = [(hit & (cell == b)).astype(F32).astype(BF) for b in range(2)]
    pick2 = jnp.concatenate(picks, axis=0)
    left = [[[], []], [[], []]]
    for p2 in range(2):
        for h in range(HEADS):
            both = mm(pick2, cut[h, p2]).astype(BF)
            for b in range(2):
                left[b][p2].append(both[b * n : (b + 1) * n])
    left = [[jnp.concatenate(x, axis=0) for x in y] for y in left]
    m = iota((1, WIN), 1)
    cp2 = (m * 171) >> 12
    u = m - cp2 * COL
    r2 = 2 * (u >> 3) + ((u >> 2) & 1)
    j2 = 2 * cp2 + (((u >> 1) & 1) ^ block)
    p2m = (u & 1) ^ block
    i2 = jnp.where(r2 >= t, r2 - t, r2 - t + WLAT)
    place = i2 * (2 * WLON - 1) + (WLON - 1) - j2
    k = iota((SPAN, WIN), 0)
    mask = None
    if block:
        o = iota((n, WIN), 0)
        lw = (o >= COL).astype(jnp.int32)
        q = o - COL * lw
        r1 = 2 * (q >> 3) + ((q >> 2) & 1)
        south = r1 >= t
        edge = (south & (lat == lats - 1)) | (~south & (lat == 0))
        dead = (lw == 1) & (((q & 1) ^ block) != p2m)
        dead = dead | (edge & ((r1 < t) != (r2 < t)))
        mask = jnp.where(dead, NEG, 0.0).astype(F32)
        mask = jnp.concatenate([mask] * HEADS, axis=0)
    for cp1 in range(PAIRS):
        acc = None
        for b in range(2):
            j1 = 2 * cp1 + (b ^ block)
            for p2 in range(2):
                target = jnp.where(p2m == p2, place + j1, -1)
                pick = (k == target).astype(F32).astype(BF)
                term = mm(left[b][p2], pick)
                acc = term if acc is None else acc + term
        acc = acc * LOG2E
        if block:
            acc = acc + mask
        for h in range(HEADS):
            for lw in range(2):
                out_ref[lw, h, cp1] = acc[(2 * h + lw) * COL : (2 * h + lw + 1) * COL]


VM = pl.BlockSpec(memory_space=pltpu.VMEM)
SM = pl.BlockSpec(memory_space=pltpu.SMEM)


BIAS_SHAPE = (2, HEADS, PAIRS, COL, WIN)
CUT_SHAPE = (HEADS, 2, 2 * WLAT * 16, SPAN)


def ffn(block, mid, up, down, step):
    h_in = norm(mid).astype(BF)
    out = mid
    for f in range(0, FF, step):
        hid = gelu(mm(h_in, up[block, :, f : f + step])).astype(BF)
        out = out + mm_nt(hid, down[block, :, f : f + step])
    return out.astype(BF).astype(F32)


def weights_of(z):
    return jnp.exp2(z - jnp.max(z, axis=-1, keepdims=True)).astype(BF)


def split_point(rows):
    return (rows // 2 + 15) // 16 * 16


def fold(y):
    rows = y.shape[0]
    half = split_point(rows)
    tail = jnp.concatenate([y[half:, 128:], jnp.zeros((2 * half - rows, 64), F32)], axis=0)
    high = jnp.concatenate([y[:half, 128:], tail], axis=1)
    return jnp.concatenate([y[:, :128], high], axis=0).astype(BF)


def unfold(data, rows):
    half = data.shape[0] - rows
    high = jnp.concatenate([data[rows:, :64], data[rows : 2 * rows - half, 64:]], axis=0)
    return jnp.concatenate([data[:rows], high], axis=1)


def tiles_of(ref, rp, k):
    two = jnp.concatenate(
        [ref[2 * rp + d, :, 2 * k * C : 2 * (k + 1) * C].astype(F32) for d in range(2)], axis=0
    )
    a, b = two[:, :C], two[:, C:]
    low = (iota((TILE, 1), 0) & 3) < 2
    return jnp.where(low, a, pltpu.roll(b, 2, 0)), jnp.where(low, pltpu.roll(a, 6, 0), b)


def project(x, w, block, at):
    return mm(x, w[block, :, at * C : (at + 1) * C])


def attend0(wins, step, bias, wqkv, wproj, up, down, x_s, q_s, k_s, v_s, acc_s):
    n = x_s.shape[1] * COL
    v_s[:, C:] = jnp.ones((2 * n, WIDE - C), BF)
    outs = []
    for lw in range(2):
        at = slice(lw * n, (lw + 1) * n)
        xn = norm(x_s[lw].reshape(n, C)).astype(BF)
        q_s[at, :] = (project(xn, wqkv, 0, 0) * (HEAD_DIM**-0.5 * LOG2E)).astype(BF)
        k_s[at, :] = project(xn, wqkv, 0, 1).astype(BF)
        v_s[at, :C] = project(xn, wqkv, 0, 2).astype(BF)
    for lw in range(2):
        done, base = 0, []
        for first, skip in wins:
            at = lw * n + first * COL
            rows = WIN - skip * COL
            q = q_s[at : at + WIN, :]
            if skip:
                q = q.astype(F32)[skip * COL :].astype(BF)
            scores = qk(q, k_s[at : at + WIN, :])
            v = v_s[at : at + WIN, :]
            acc = None
            for h in range(HEADS):
                z = scores[h] + bias[lw, h, skip:].reshape(rows, WIN)
                term = mm(weights_of(z), v * value_mask(h))
                acc = term if acc is None else acc + term
            acc_s[done : done + rows, :] = acc
            done += rows
            base.append(x_s[lw, first + skip : first + PAIRS].reshape(rows, C))
        att = mm(divide(acc_s[:done, :]), wproj[0])
        outs.append(ffn(0, jnp.concatenate(base, axis=0) + att, up, down, step))
    return outs


def own_kernel(
    x, bias, wqkv, wproj, up, down, f_ref, n_ref, x_s, q_s, k_s, v_s, acc_s,
):
    cps = x_s.shape[1]
    for cp in range(cps):
        for rp in range(RPS):
            x_s[0, cp, rp], x_s[1, cp, rp] = tiles_of(x, rp, cp)
    wins = [(i, 0) for i in range(0, cps, PAIRS)]
    outs = attend0(wins, FF, bias, wqkv, wproj, up, down, x_s, q_s, k_s, v_s, acc_s)
    for lw in range(2):
        f_ref[lw] = outs[lw].reshape(cps, RPS, TILE, C)
        n_ref[lw] = norm(outs[lw]).reshape(cps, RPS, TILE, C)


def edge_kernel(
    east, west, bias, n_own, wqkv, wproj, up, down,
    ext_ref, up_ref, dn_ref, x_s, q_s, k_s, v_s, acc_s,
):
    own = n_own.shape[1]
    for cp in range(2 * PAIRS):
        ref, k = (east, cp) if cp < PAIRS else (west, own - 2 * PAIRS + cp)
        for rp in range(RPS):
            x_s[0, cp, rp], x_s[1, cp, rp] = tiles_of(ref, rp, k)
    wins = [(0, 0), (PAIRS, PAIRS - 1)]
    outs = attend0(wins, 256, bias, wqkv, wproj, up, down, x_s, q_s, k_s, v_s, acc_s)
    side = [norm(o).reshape(-1, RPS, TILE, C) for o in outs]
    _, cell, level = tile_bits((1, 1, TILE, 1), 2)
    keep = [level == 1, level == 0]
    for w in range(2):
        pick = lambda a: jnp.where(keep[w], a[0], a[1])
        beside = pick(side)
        o = jnp.concatenate([beside[PAIRS:], pick(n_own), beside[:PAIRS]], axis=0)
        ext_ref[w] = jnp.where(cell == 0, o[1:], o[:-1])
    e = [ext_ref[w] for w in range(2)]
    top = (iota((1, TILE, 1), 1)) < 4
    flat = lambda a: a.reshape(-1, C)
    roll4 = lambda a: pltpu.roll(a, 4, 1)
    half = jnp.where(top, e[0][:, 2], roll4(e[1][:, 2]))
    up_ref[...] = fold(jnp.concatenate([flat(e[0][:, :2]), flat(e[1][:, :2]), flat(half)], axis=0))
    half = jnp.where(top, roll4(e[1][:, 0]), e[0][:, 0])
    dn_ref[...] = fold(jnp.concatenate([flat(e[0][:, 1:]), flat(e[1][:, 1:]), flat(half)], axis=0))


def row_of_tile():
    shape = (1, RPS, TILE, 1)
    return 2 * iota(shape, 1) + tile_bits(shape, 2)[0]


def tiles(a):
    return a.reshape(-1, RPS, TILE, a.shape[-1])


def same_side(t):
    def south(m):
        u = m - ((m * 171) >> 12) * COL
        return (2 * (u >> 3) + ((u >> 2) & 1) >= t).astype(jnp.int32)

    return south(iota((WIN, WIN), 0)) == south(iota((WIN, WIN), 1))


def late_rows():
    return ((iota((COL, 1), 0) >> 1) & 1) == 1


def swap_top(scores, edge):
    top = jnp.where(late_rows(), edge, scores[:COL])
    return jnp.concatenate([top, scores[COL:]], axis=0)


def ready_kernel(sh, sc, tab, ext, f_own, wqkv, z_ref, f_ref, v_ref, q_ref, bias, cut, k_s):
    own = q_ref.shape[0] // 2 // COL
    n = ext.shape[1] * COL
    _, cell, level = tile_bits((1, 1, TILE, 1), 2)
    for w in range(2):
        mine = jnp.where(level == 1 - w, f_own[0], f_own[1])
        before = jnp.concatenate([mine[own - 1 :], mine[: own - 1]], axis=0)
        f_ref[w] = jnp.where(cell == 0, mine, before)
        x = ext[w].reshape(n, C).astype(BF)
        k_s[w * n : (w + 1) * n, :] = project(x, wqkv, 1, 1).astype(BF)
        v_ref[w * n : (w + 1) * n, :] = project(x, wqkv, 1, 2)
        fix = jnp.where(cell == 0, ext[w, :1], ext[w, own : own + 1])
        x = jnp.concatenate([fix, ext[w, 1:own]], axis=0).reshape(-1, C).astype(BF)
        q = project(x, wqkv, 1, 0) * (HEAD_DIM**-0.5 * LOG2E)
        q_ref[w * own * COL : (w + 1) * own * COL, :] = q.astype(BF)
    build_bias(1, sh[0], sc, tab, bias, cut)
    same = same_side(sh[0])
    last = own // PAIRS
    for w in range(2):
        for i in range(last):
            q = q_ref[w * own * COL + i * WIN : w * own * COL + (i + 1) * WIN, :]
            pick = lambda j: k_s[w * n + j * WIN : w * n + (j + 1) * WIN, :]
            scores = qk(q, pick(i))
            if i == 0:
                edge = qk(q.astype(F32)[:COL].astype(BF), pick(last))
                scores = [swap_top(a, b) for a, b in zip(scores, edge)]
            for h in range(HEADS):
                z_ref[w, i, h] = jnp.where(same, scores[h], 0.0) + bias[w, h].reshape(WIN, WIN)


def second_kernel(
    sh, f1, above, below, z_ref, v_own, q_ref, wqkv, wproj, up, down,
    out, k_s, vs_s, vn_s, r_s, acc_s,
):
    t = sh[0]
    own = f1.shape[1]
    n = v_own.shape[0] // 2
    wide = n // COL
    south = unfold(below[...].astype(F32), 2 * wide * 20)
    north = unfold(above[...].astype(F32), 2 * wide * 20)
    full = wide * 16
    roll4 = lambda a: pltpu.roll(a, 4, 1)

    def halves(y):
        rest = y[2 * full :].reshape(wide, TILE, C)
        return [y[w * full : (w + 1) * full].reshape(wide, 2, TILE, C) for w in range(2)], rest

    (s_full, s_half), (n_full, n_half) = halves(south), halves(north)
    lower = row_of_tile() >= t
    cell = tile_bits((1, 1, TILE, 1), 2)[1]
    for w in range(2):
        low = jnp.concatenate(
            [s_full[w], (roll4(s_half) if w else s_half)[:, None]], axis=1)
        high = jnp.concatenate(
            [(roll4(n_half) if w else n_half)[:, None], n_full[w]], axis=1)
        x = jnp.where(lower, high, low).reshape(n, C).astype(BF)
        at = slice(w * n, (w + 1) * n)
        k_s[at, :] = project(x, wqkv, 1, 1).astype(BF)
        mine, other = tiles(v_own[at, :]), tiles(project(x, wqkv, 1, 2))
        vs_s[at, :C] = jnp.where(lower, mine, other).reshape(n, C).astype(BF)
        vn_s[at, :C] = jnp.where(lower, other, mine).reshape(n, C).astype(BF)
    vs_s[:, C:] = vn_s[:, C:] = jnp.ones((2 * n, WIDE - C), BF)
    same = same_side(t)
    last = own // PAIRS
    for w in range(2):
        for i in range(own // PAIRS):
            at = slice(w * own * COL + i * WIN, w * own * COL + (i + 1) * WIN)
            q = q_ref[at, :]
            pick = lambda ref, j: ref[w * n + j * WIN : w * n + (j + 1) * WIN, :]
            scores = qk(q, pick(k_s, i))
            vs, vn = pick(vs_s, i), pick(vn_s, i)
            if i == 0:
                edge = qk(q.astype(F32)[:COL].astype(BF), pick(k_s, last))
                scores = [swap_top(a, b) for a, b in zip(scores, edge)]
                vs2, vn2 = pick(vs_s, last), pick(vn_s, last)
                fix_s, fix_n = jnp.zeros((COL, WIDE), F32), jnp.zeros((COL, WIDE), F32)
            sum_s = sum_n = None
            for h in range(HEADS):
                p = weights_of(z_ref[w, i, h] + jnp.where(same, 0.0, scores[h]))
                hm = value_mask(h)
                ts, tn = mm(p, vs * hm), mm(p, vn * hm)
                sum_s = ts if sum_s is None else sum_s + ts
                sum_n = tn if sum_n is None else sum_n + tn
                if i == 0:
                    p2 = p.astype(F32)[:COL].astype(BF)
                    fix_s = fix_s + mm(p2, vs2 * hm)
                    fix_n = fix_n + mm(p2, vn2 * hm)
            acc = jnp.where(lower, tiles(sum_s), tiles(sum_n))
            if i == 0:
                fix = jnp.where(lower, tiles(fix_s), tiles(fix_n))
                acc = jnp.concatenate([jnp.where(cell == 0, acc[:1], fix), acc[1:]], axis=0)
            acc_s[i * WIN : (i + 1) * WIN, :] = acc.reshape(WIN, WIDE)
        att = mm(divide(acc_s[...]), wproj[1])
        r_s[w] = tiles(ffn(1, f1[w].reshape(-1, C) + att, up, down, FF))
    low = (iota((TILE, 1), 0) & 3) < 2
    _, cell, level = tile_bits((TILE, 1), 0)
    for k in range(own):
        nxt = (k + 1) % own
        for rp in range(RPS):
            n0, n1 = (jnp.where(cell == 0, r_s[w, k, rp], r_s[w, nxt, rp]) for w in range(2))
            t0, t1 = jnp.where(level == 1, n0, n1), jnp.where(level == 0, n0, n1)
            a = jnp.where(low, t0, pltpu.roll(t1, 2, 0))
            b = jnp.where(low, pltpu.roll(t0, 6, 0), t1)
            pair = jnp.concatenate([a, b], axis=1)
            for d in range(2):
                out[2 * rp + d, :, 2 * k * C : 2 * (k + 1) * C] = pair[4 * d : 4 * d + 4].astype(BF)


VM = pl.BlockSpec(memory_space=pltpu.VMEM)
SM = pl.BlockSpec(memory_space=pltpu.SMEM)


def call(kernel, scalars, args, outs, scratch, name, flops):
    return pl.pallas_call(
        kernel,
        out_shape=outs,
        in_specs=[SM] * len(scalars) + [VM] * len(args),
        out_specs=[VM] * len(outs),
        scratch_shapes=scratch,
        compiler_params=pltpu.CompilerParams(vmem_limit_bytes=24 * 2**20),
        cost_estimate=pl.CostEstimate(
            flops=flops, bytes_accessed=4 * 10**6, transcendentals=10**6
        ),
        name=name,
    )(*scalars, *args)


def shifted(x, axis, by):
    size = lax.axis_size(axis)
    return lax.ppermute(x, axis, [(i, (i + by) % size) for i in range(size)])


def body(field, shift, window_type, qkv_weight, proj_weight, up_weight, down_weight, bias_table):
    own = field.shape[2] // C // 2
    wide = own + PAIRS
    x = field.transpose(1, 0, 2)
    weights = (qkv_weight, proj_weight, up_weight, down_weight.transpose(0, 2, 1))
    table = bias_table.transpose(0, 2, 1, 3)
    row = iota((3, window_type.shape[1]), 0)
    scalars = jnp.where(
        row == 2, lax.axis_index("lat"), jnp.pad(window_type, ((0, 1), (0, 0))))
    east = shifted(x, "lon", -1)
    west = shifted(x, "lon", 1)
    sds = jax.ShapeDtypeStruct
    rows = 2 * wide * 20
    pay = (rows + split_point(rows), 128)
    tile = lambda cps: (2, cps, RPS, TILE, C)
    cut = pltpu.VMEM(CUT_SHAPE, BF)

    def scratch(cps, rows):
        n = 2 * cps * COL
        return [pltpu.VMEM(tile(cps), F32), pltpu.VMEM((n, C), BF), pltpu.VMEM((n, C), BF),
                pltpu.VMEM((n, WIDE), BF), pltpu.VMEM((rows, WIDE), F32)]

    (bias0,) = call(
        functools.partial(build_bias, 0, 0), (scalars,), (table,), [sds(BIAS_SHAPE, F32)], [cut],
        "bias0", 10**9)
    f_own, n_own = call(
        own_kernel, (), (x, bias0) + weights, [sds(tile(own), F32), sds(tile(own), F32)],
        scratch(own, own * COL), "own0", 2 * 10**9)
    ext, pay_up, pay_dn = call(
        edge_kernel, (), (east, west, bias0, n_own) + weights,
        [sds(tile(wide), F32), sds(pay, BF), sds(pay, BF)],
        scratch(2 * PAIRS, WIN + COL), "edge0", 2 * 10**9)
    below = shifted(pay_up, "lat", -1)
    above = shifted(pay_dn, "lat", 1)
    m, n = 2 * wide * COL, 2 * own * COL
    z_shape = (2, own // PAIRS, HEADS, WIN, WIN)
    z1, f1, v_own, q1 = call(
        ready_kernel, (shift, scalars), (table, ext, f_own, qkv_weight),
        [sds(z_shape, F32), sds(tile(own), F32), sds((m, C), F32), sds((n, C), BF)],
        [pltpu.VMEM(BIAS_SHAPE, F32), cut, pltpu.VMEM((m, C), BF)], "ready1", 2 * 10**9)
    (out,) = call(
        second_kernel, (shift,), (f1, above, below, z1, v_own, q1) + weights,
        [sds(x.shape, BF)],
        [pltpu.VMEM((m, lanes), BF) for lanes in (C, WIDE, WIDE)]
        + [pltpu.VMEM(tile(own), F32), pltpu.VMEM((own * COL, WIDE), F32)],
        "block1", 2 * 10**9)
    return out.transpose(1, 0, 2)


def solution(mesh):
    return jax.shard_map(
        body,
        mesh=mesh,
        in_specs=(P(None, "lat", "lon"), P(), P(), P(), P(), P(), P(), P()),
        out_specs=P(None, "lat", "lon"),
        check_vma=False,
    )
```

```python
import functools

import jax
import jax.numpy as jnp
from jax import lax
from jax.experimental import pallas as pl
from jax.experimental.pallas import tpu as pltpu
from jax.sharding import PartitionSpec as P


HEADS = 6
HEAD_DIM = 32
C = 192
FF = 768
WLAT = 6
WLON = 12
TILE = 8
PAIRS = WLON // 2
RPS = WLAT // 2
COL = RPS * TILE
WIN = PAIRS * COL
SPAN = WLAT * (2 * WLON - 1)
NEG = -1e30
LOG2E = 1.4426950408889634
F32 = jnp.float32
BF = jnp.bfloat16


def mm(a, b):
    return jnp.dot(a, b, preferred_element_type=F32)


def mm_nt(a, b):
    return lax.dot_general(a, b, (((1,), (1,)), ((), ())), preferred_element_type=F32)


def norm(x):
    center = x - jnp.mean(x, axis=-1, keepdims=True)
    spread = mm((center * center).astype(BF), jnp.ones((C, C), BF)) * (1.0 / C)
    return center * lax.rsqrt(spread + 1e-05)


def gelu(x):
    return 0.5 * x * (1.0 + lax.erf(x * 0.7071067811865476))


def iota(shape, dim):
    return lax.broadcasted_iota(jnp.int32, shape, dim)


def qk(q, k):
    n = q.shape[0]
    parts = []
    for lo, hi in ((0, 128), (128, C)):
        lane = iota((1, hi - lo), 1)
        stack = []
        for h in range((hi - lo) // HEAD_DIM):
            hit = (lane >= h * HEAD_DIM) & (lane < (h + 1) * HEAD_DIM)
            stack.append(q[:, lo:hi] * hit.astype(F32).astype(BF))
        res = mm_nt(jnp.concatenate(stack, axis=0), k[:, lo:hi])
        parts += [res[h * n : (h + 1) * n] for h in range(len(stack))]
    return parts


WIDE = 256


def value_mask(h):
    lane = iota((1, WIDE), 1)
    hit = (lane >= h * HEAD_DIM) & (lane < (h + 1) * HEAD_DIM) | (lane == C + h)
    if h == 0:
        hit = hit | (lane >= C + HEADS)
    return hit.astype(F32).astype(BF)


def divide(acc):
    tail = acc[:, 128:]
    inv = 1.0 / jnp.where(iota((1, 128), 1) >= 64, tail, 1.0)
    high = inv.astype(BF)
    low = (inv - high.astype(F32)).astype(BF)
    i, lane = iota((128, C), 0), iota((128, C), 1)
    first = (i - 64) * HEAD_DIM
    spread = ((lane >= first) & (lane < first + HEAD_DIM)).astype(F32).astype(BF)
    return (acc[:, :C] * (mm(high, spread) + mm(low, spread))).astype(BF)


def tile_bits(shape, dim):
    s = iota(shape, dim)
    return s >> 2, (s >> 1) & 1, s & 1


def build_bias(block, t, sc, tab, out_ref, cut):
    lat, lats = sc[2, 0], sc.shape[1]
    for h in range(HEADS):
        rows = tab[h].astype(F32)
        for p1 in range(2):
            for p2 in range(2):
                for i1 in range(WLAT):
                    a = ((p1 * 2 + p2) * WLAT + i1) * SPAN
                    at = (p1 * WLAT + i1) * 16
                    cut[h, p2, at : at + 16, :] = rows[:, a : a + SPAN].astype(BF)
    n, src = 2 * COL, 2 * WLAT * 16
    o, s = iota((n, src), 0), iota((n, src), 1)
    lw = (o >= COL).astype(jnp.int32)
    q = o - COL * lw
    r1 = 2 * (q >> 3) + ((q >> 2) & 1)
    p1 = (q & 1) ^ block
    own = r1 >= t
    i1 = jnp.where(own, r1 - t, r1 - t + WLAT)
    north = lax.rem(lat + lats - 1, lats)
    kind = jnp.where(
        lw == 0,
        jnp.where(own, sc[0, lat], sc[0, north]),
        jnp.where(own, sc[1, lat], sc[1, north]),
    )
    hit = s == (p1 * WLAT + i1) * 16 + kind
    cell = (q >> 1) & 1
    picks = [(hit & (cell == b)).astype(F32).astype(BF) for b in range(2)]
    pick2 = jnp.concatenate(picks, axis=0)
    left = [[[], []], [[], []]]
    for p2 in range(2):
        for h in range(HEADS):
            both = mm(pick2, cut[h, p2]).astype(BF)
            for b in range(2):
                left[b][p2].append(both[b * n : (b + 1) * n])
    left = [[jnp.concatenate(x, axis=0) for x in y] for y in left]
    m = iota((1, WIN), 1)
    cp2 = (m * 171) >> 12
    u = m - cp2 * COL
    r2 = 2 * (u >> 3) + ((u >> 2) & 1)
    j2 = 2 * cp2 + (((u >> 1) & 1) ^ block)
    p2m = (u & 1) ^ block
    i2 = jnp.where(r2 >= t, r2 - t, r2 - t + WLAT)
    place = i2 * (2 * WLON - 1) + (WLON - 1) - j2
    k = iota((SPAN, WIN), 0)
    mask = None
    if block:
        o = iota((n, WIN), 0)
        lw = (o >= COL).astype(jnp.int32)
        q = o - COL * lw
        r1 = 2 * (q >> 3) + ((q >> 2) & 1)
        south = r1 >= t
        edge = (south & (lat == lats - 1)) | (~south & (lat == 0))
        dead = (lw == 1) & (((q & 1) ^ block) != p2m)
        dead = dead | (edge & ((r1 < t) != (r2 < t)))
        mask = jnp.where(dead, NEG, 0.0).astype(F32)
        mask = jnp.concatenate([mask] * HEADS, axis=0)
    for cp1 in range(PAIRS):
        acc = None
        for b in range(2):
            j1 = 2 * cp1 + (b ^ block)
            for p2 in range(2):
                target = jnp.where(p2m == p2, place + j1, -1)
                pick = (k == target).astype(F32).astype(BF)
                term = mm(left[b][p2], pick)
                acc = term if acc is None else acc + term
        acc = acc * LOG2E
        if block:
            acc = acc + mask
        for h in range(HEADS):
            for lw in range(2):
                out_ref[lw, h, cp1] = acc[(2 * h + lw) * COL : (2 * h + lw + 1) * COL]


VM = pl.BlockSpec(memory_space=pltpu.VMEM)
SM = pl.BlockSpec(memory_space=pltpu.SMEM)


BIAS_SHAPE = (2, HEADS, PAIRS, COL, WIN)
CUT_SHAPE = (HEADS, 2, 2 * WLAT * 16, SPAN)


def ffn(block, mid, up, down, step):
    h_in = norm(mid).astype(BF)
    out = mid
    for f in range(0, FF, step):
        hid = gelu(mm(h_in, up[block, :, f : f + step])).astype(BF)
        out = out + mm_nt(hid, down[block, :, f : f + step])
    return out.astype(BF).astype(F32)


def weights_of(z):
    return jnp.exp2(z - jnp.max(z, axis=-1, keepdims=True)).astype(BF)


def split_point(rows):
    return (rows // 2 + 15) // 16 * 16


def fold(y):
    rows = y.shape[0]
    half = split_point(rows)
    tail = jnp.concatenate([y[half:, 128:], jnp.zeros((2 * half - rows, 64), F32)], axis=0)
    high = jnp.concatenate([y[:half, 128:], tail], axis=1)
    return jnp.concatenate([y[:, :128], high], axis=0).astype(BF)


def unfold(data, rows):
    half = data.shape[0] - rows
    high = jnp.concatenate([data[rows:, :64], data[rows : 2 * rows - half, 64:]], axis=0)
    return jnp.concatenate([data[:rows], high], axis=1)


def tiles_of(ref, rp, k):
    two = jnp.concatenate(
        [ref[2 * rp + d, :, 2 * k * C : 2 * (k + 1) * C].astype(F32) for d in range(2)], axis=0
    )
    a, b = two[:, :C], two[:, C:]
    low = (iota((TILE, 1), 0) & 3) < 2
    return jnp.where(low, a, pltpu.roll(b, 2, 0)), jnp.where(low, pltpu.roll(a, 6, 0), b)


def project(x, w, block, at):
    return mm(x, w[block, :, at * C : (at + 1) * C])


def attend0(wins, step, bias, wqkv, wproj, up, down, x_s, q_s, k_s, v_s, acc_s):
    n = x_s.shape[1] * COL
    v_s[:, C:] = jnp.ones((2 * n, WIDE - C), BF)
    outs = []
    for lw in range(2):
        at = slice(lw * n, (lw + 1) * n)
        xn = norm(x_s[lw].reshape(n, C)).astype(BF)
        q_s[at, :] = (project(xn, wqkv, 0, 0) * (HEAD_DIM**-0.5 * LOG2E)).astype(BF)
        k_s[at, :] = project(xn, wqkv, 0, 1).astype(BF)
        v_s[at, :C] = project(xn, wqkv, 0, 2).astype(BF)
    for lw in range(2):
        done, base = 0, []
        for first, skip in wins:
            at = lw * n + first * COL
            rows = WIN - skip * COL
            q = q_s[at : at + WIN, :]
            if skip:
                q = q.astype(F32)[skip * COL :].astype(BF)
            scores = qk(q, k_s[at : at + WIN, :])
            v = v_s[at : at + WIN, :]
            acc = None
            for h in range(HEADS):
                z = scores[h] + bias[lw, h, skip:].reshape(rows, WIN)
                term = mm(weights_of(z), v * value_mask(h))
                acc = term if acc is None else acc + term
            acc_s[done : done + rows, :] = acc
            done += rows
            base.append(x_s[lw, first + skip : first + PAIRS].reshape(rows, C))
        att = mm(divide(acc_s[:done, :]), wproj[0])
        outs.append(ffn(0, jnp.concatenate(base, axis=0) + att, up, down, step))
    return outs


def own_kernel(
    x, bias, wqkv, wproj, up, down, f_ref, n_ref, x_s, q_s, k_s, v_s, acc_s,
):
    cps = x_s.shape[1]
    for cp in range(cps):
        for rp in range(RPS):
            x_s[0, cp, rp], x_s[1, cp, rp] = tiles_of(x, rp, cp)
    wins = [(i, 0) for i in range(0, cps, PAIRS)]
    outs = attend0(wins, FF, bias, wqkv, wproj, up, down, x_s, q_s, k_s, v_s, acc_s)
    for lw in range(2):
        f_ref[lw] = outs[lw].reshape(cps, RPS, TILE, C)
        n_ref[lw] = norm(outs[lw]).reshape(cps, RPS, TILE, C)


def edge_kernel(
    east, west, bias, n_own, wqkv, wproj, up, down,
    ext_ref, up_ref, dn_ref, x_s, q_s, k_s, v_s, acc_s,
):
    own = n_own.shape[1]
    for cp in range(2 * PAIRS):
        ref, k = (east, cp) if cp < PAIRS else (west, own - 2 * PAIRS + cp)
        for rp in range(RPS):
            x_s[0, cp, rp], x_s[1, cp, rp] = tiles_of(ref, rp, k)
    wins = [(0, 0), (PAIRS, PAIRS - 1)]
    outs = attend0(wins, 256, bias, wqkv, wproj, up, down, x_s, q_s, k_s, v_s, acc_s)
    side = [norm(o).reshape(-1, RPS, TILE, C) for o in outs]
    _, cell, level = tile_bits((1, 1, TILE, 1), 2)
    keep = [level == 1, level == 0]
    for w in range(2):
        pick = lambda a: jnp.where(keep[w], a[0], a[1])
        beside = pick(side)
        o = jnp.concatenate([beside[PAIRS:], pick(n_own), beside[:PAIRS]], axis=0)
        ext_ref[w] = jnp.where(cell == 0, o[1:], o[:-1])
    e = [ext_ref[w] for w in range(2)]
    top = (iota((1, TILE, 1), 1)) < 4
    flat = lambda a: a.reshape(-1, C)
    roll4 = lambda a: pltpu.roll(a, 4, 1)
    half = jnp.where(top, e[0][:, 2], roll4(e[1][:, 2]))
    up_ref[...] = fold(jnp.concatenate([flat(e[0][:, :2]), flat(e[1][:, :2]), flat(half)], axis=0))
    half = jnp.where(top, roll4(e[1][:, 0]), e[0][:, 0])
    dn_ref[...] = fold(jnp.concatenate([flat(e[0][:, 1:]), flat(e[1][:, 1:]), flat(half)], axis=0))


def row_of_tile():
    shape = (1, RPS, TILE, 1)
    return 2 * iota(shape, 1) + tile_bits(shape, 2)[0]


def tiles(a):
    return a.reshape(-1, RPS, TILE, a.shape[-1])


def same_side(t):
    def south(m):
        u = m - ((m * 171) >> 12) * COL
        return (2 * (u >> 3) + ((u >> 2) & 1) >= t).astype(jnp.int32)

    return south(iota((WIN, WIN), 0)) == south(iota((WIN, WIN), 1))


def late_rows():
    return ((iota((COL, 1), 0) >> 1) & 1) == 1


def swap_top(scores, edge):
    top = jnp.where(late_rows(), edge, scores[:COL])
    return jnp.concatenate([top, scores[COL:]], axis=0)


def ready_kernel(sh, sc, tab, ext, f_own, wqkv, z_ref, f_ref, v_ref, q_ref, bias, cut, k_s):
    own = q_ref.shape[0] // 2 // COL
    n = ext.shape[1] * COL
    _, cell, level = tile_bits((1, 1, TILE, 1), 2)
    for w in range(2):
        mine = jnp.where(level == 1 - w, f_own[0], f_own[1])
        before = jnp.concatenate([mine[own - 1 :], mine[: own - 1]], axis=0)
        f_ref[w] = jnp.where(cell == 0, mine, before)
        x = ext[w].reshape(n, C).astype(BF)
        k_s[w * n : (w + 1) * n, :] = project(x, wqkv, 1, 1).astype(BF)
        v_ref[w * n : (w + 1) * n, :] = project(x, wqkv, 1, 2)
        fix = jnp.where(cell == 0, ext[w, :1], ext[w, own : own + 1])
        x = jnp.concatenate([fix, ext[w, 1:own]], axis=0).reshape(-1, C).astype(BF)
        q = project(x, wqkv, 1, 0) * (HEAD_DIM**-0.5 * LOG2E)
        q_ref[w * own * COL : (w + 1) * own * COL, :] = q.astype(BF)
    build_bias(1, sh[0], sc, tab, bias, cut)
    same = same_side(sh[0])
    last = own // PAIRS
    for w in range(2):
        for i in range(last):
            q = q_ref[w * own * COL + i * WIN : w * own * COL + (i + 1) * WIN, :]
            pick = lambda j: k_s[w * n + j * WIN : w * n + (j + 1) * WIN, :]
            scores = qk(q, pick(i))
            if i == 0:
                edge = qk(q.astype(F32)[:COL].astype(BF), pick(last))
                scores = [swap_top(a, b) for a, b in zip(scores, edge)]
            for h in range(HEADS):
                z_ref[w, i, h] = jnp.where(same, scores[h], 0.0) + bias[w, h].reshape(WIN, WIN)


def second_kernel(
    sh, f1, above, below, z_ref, v_own, q_ref, wqkv, wproj, up, down,
    out, k_s, vs_s, vn_s, r_s, acc_s,
):
    t = sh[0]
    own = f1.shape[1]
    n = v_own.shape[0] // 2
    wide = n // COL
    south = unfold(below[...].astype(F32), 2 * wide * 20)
    north = unfold(above[...].astype(F32), 2 * wide * 20)
    full = wide * 16
    roll4 = lambda a: pltpu.roll(a, 4, 1)

    def halves(y):
        rest = y[2 * full :].reshape(wide, TILE, C)
        return [y[w * full : (w + 1) * full].reshape(wide, 2, TILE, C) for w in range(2)], rest

    (s_full, s_half), (n_full, n_half) = halves(south), halves(north)
    lower = row_of_tile() >= t
    cell = tile_bits((1, 1, TILE, 1), 2)[1]
    for w in range(2):
        low = jnp.concatenate(
            [s_full[w], (roll4(s_half) if w else s_half)[:, None]], axis=1)
        high = jnp.concatenate(
            [(roll4(n_half) if w else n_half)[:, None], n_full[w]], axis=1)
        x = jnp.where(lower, high, low).reshape(n, C).astype(BF)
        at = slice(w * n, (w + 1) * n)
        k_s[at, :] = project(x, wqkv, 1, 1).astype(BF)
        mine, other = tiles(v_own[at, :]), tiles(project(x, wqkv, 1, 2))
        vs_s[at, :C] = jnp.where(lower, mine, other).reshape(n, C).astype(BF)
        vn_s[at, :C] = jnp.where(lower, other, mine).reshape(n, C).astype(BF)
    vs_s[:, C:] = vn_s[:, C:] = jnp.ones((2 * n, WIDE - C), BF)
    same = same_side(t)
    last = own // PAIRS
    for w in range(2):
        for i in range(own // PAIRS):
            at = slice(w * own * COL + i * WIN, w * own * COL + (i + 1) * WIN)
            q = q_ref[at, :]
            pick = lambda ref, j: ref[w * n + j * WIN : w * n + (j + 1) * WIN, :]
            scores = qk(q, pick(k_s, i))
            vs, vn = pick(vs_s, i), pick(vn_s, i)
            if i == 0:
                edge = qk(q.astype(F32)[:COL].astype(BF), pick(k_s, last))
                scores = [swap_top(a, b) for a, b in zip(scores, edge)]
                vs2, vn2 = pick(vs_s, last), pick(vn_s, last)
                fix_s, fix_n = jnp.zeros((COL, WIDE), F32), jnp.zeros((COL, WIDE), F32)
            sum_s = sum_n = None
            for h in range(HEADS):
                p = weights_of(z_ref[w, i, h] + jnp.where(same, 0.0, scores[h]))
                hm = value_mask(h)
                ts, tn = mm(p, vs * hm), mm(p, vn * hm)
                sum_s = ts if sum_s is None else sum_s + ts
                sum_n = tn if sum_n is None else sum_n + tn
                if i == 0:
                    p2 = p.astype(F32)[:COL].astype(BF)
                    fix_s = fix_s + mm(p2, vs2 * hm)
                    fix_n = fix_n + mm(p2, vn2 * hm)
            acc = jnp.where(lower, tiles(sum_s), tiles(sum_n))
            if i == 0:
                fix = jnp.where(lower, tiles(fix_s), tiles(fix_n))
                acc = jnp.concatenate([jnp.where(cell == 0, acc[:1], fix), acc[1:]], axis=0)
            acc_s[i * WIN : (i + 1) * WIN, :] = acc.reshape(WIN, WIDE)
        att = mm(divide(acc_s[...]), wproj[1])
        r_s[w] = tiles(ffn(1, f1[w].reshape(-1, C) + att, up, down, FF))
    low = (iota((TILE, 1), 0) & 3) < 2
    _, cell, level = tile_bits((TILE, 1), 0)
    for k in range(own):
        nxt = (k + 1) % own
        for rp in range(RPS):
            n0, n1 = (jnp.where(cell == 0, r_s[w, k, rp], r_s[w, nxt, rp]) for w in range(2))
            t0, t1 = jnp.where(level == 1, n0, n1), jnp.where(level == 0, n0, n1)
            a = jnp.where(low, t0, pltpu.roll(t1, 2, 0))
            b = jnp.where(low, pltpu.roll(t0, 6, 0), t1)
            pair = jnp.concatenate([a, b], axis=1)
            for d in range(2):
                out[2 * rp + d, :, 2 * k * C : 2 * (k + 1) * C] = pair[4 * d : 4 * d + 4].astype(BF)


VM = pl.BlockSpec(memory_space=pltpu.VMEM)
SM = pl.BlockSpec(memory_space=pltpu.SMEM)


def call(kernel, scalars, args, outs, scratch, name, flops):
    return pl.pallas_call(
        kernel,
        out_shape=outs,
        in_specs=[SM] * len(scalars) + [VM] * len(args),
        out_specs=[VM] * len(outs),
        scratch_shapes=scratch,
        compiler_params=pltpu.CompilerParams(vmem_limit_bytes=24 * 2**20),
        cost_estimate=pl.CostEstimate(
            flops=flops, bytes_accessed=4 * 10**6, transcendentals=10**6
        ),
        name=name,
    )(*scalars, *args)


def shifted(x, axis, by):
    size = lax.axis_size(axis)
    return lax.ppermute(x, axis, [(i, (i + by) % size) for i in range(size)])


def body(field, shift, window_type, qkv_weight, proj_weight, up_weight, down_weight, bias_table):
    own = field.shape[2] // C // 2
    wide = own + PAIRS
    x = field.transpose(1, 0, 2)
    weights = (qkv_weight, proj_weight, up_weight, down_weight.transpose(0, 2, 1))
    table = bias_table.transpose(0, 2, 1, 3)
    row = iota((3, window_type.shape[1]), 0)
    scalars = jnp.where(
        row == 2, lax.axis_index("lat"), jnp.pad(window_type, ((0, 1), (0, 0))))
    east = shifted(x, "lon", -1)
    west = shifted(x, "lon", 1)
    sds = jax.ShapeDtypeStruct
    rows = 2 * wide * 20
    pay = (rows + split_point(rows), 128)
    tile = lambda cps: (2, cps, RPS, TILE, C)
    cut = pltpu.VMEM(CUT_SHAPE, BF)

    def scratch(cps, rows):
        n = 2 * cps * COL
        return [pltpu.VMEM(tile(cps), F32), pltpu.VMEM((n, C), BF), pltpu.VMEM((n, C), BF),
                pltpu.VMEM((n, WIDE), BF), pltpu.VMEM((rows, WIDE), F32)]

    (bias0,) = call(
        functools.partial(build_bias, 0, 0), (scalars,), (table[0],), [sds(BIAS_SHAPE, F32)], [cut],
        "bias0", 10**9)
    f_own, n_own = call(
        own_kernel, (), (x, bias0) + weights, [sds(tile(own), F32), sds(tile(own), F32)],
        scratch(own, own * COL), "own0", 2 * 10**9)
    ext, pay_up, pay_dn = call(
        edge_kernel, (), (east, west, bias0, n_own) + weights,
        [sds(tile(wide), F32), sds(pay, BF), sds(pay, BF)],
        scratch(2 * PAIRS, WIN + COL), "edge0", 2 * 10**9)
    below = shifted(pay_up, "lat", -1)
    above = shifted(pay_dn, "lat", 1)
    m, n = 2 * wide * COL, 2 * own * COL
    z_shape = (2, own // PAIRS, HEADS, WIN, WIN)
    z1, f1, v_own, q1 = call(
        ready_kernel, (shift, scalars), (table[1], ext, f_own, qkv_weight),
        [sds(z_shape, F32), sds(tile(own), F32), sds((m, C), F32), sds((n, C), BF)],
        [pltpu.VMEM(BIAS_SHAPE, F32), cut, pltpu.VMEM((m, C), BF)], "ready1", 2 * 10**9)
    (out,) = call(
        second_kernel, (shift,), (f1, above, below, z1, v_own, q1) + weights,
        [sds(x.shape, BF)],
        [pltpu.VMEM((m, lanes), BF) for lanes in (C, WIDE, WIDE)]
        + [pltpu.VMEM(tile(own), F32), pltpu.VMEM((own * COL, WIDE), F32)],
        "block1", 2 * 10**9)
    return out.transpose(1, 0, 2)


def solution(mesh):
    return jax.shard_map(
        body,
        mesh=mesh,
        in_specs=(P(None, "lat", "lon"), P(), P(), P(), P(), P(), P(), P()),
        out_specs=P(None, "lat", "lon"),
        check_vma=False,
    )
```

```python
import functools

import jax
import jax.numpy as jnp
from jax import lax
from jax.experimental import pallas as pl
from jax.experimental.pallas import tpu as pltpu
from jax.sharding import PartitionSpec as P


HEADS = 6
HEAD_DIM = 32
C = 192
FF = 768
WLAT = 6
WLON = 12
TILE = 8
PAIRS = WLON // 2
RPS = WLAT // 2
COL = RPS * TILE
WIN = PAIRS * COL
SPAN = WLAT * (2 * WLON - 1)
NEG = -1e30
LOG2E = 1.4426950408889634
F32 = jnp.float32
BF = jnp.bfloat16


def mm(a, b):
    return jnp.dot(a, b, preferred_element_type=F32)


def mm_nt(a, b):
    return lax.dot_general(a, b, (((1,), (1,)), ((), ())), preferred_element_type=F32)


def norm(x):
    center = x - jnp.mean(x, axis=-1, keepdims=True)
    spread = mm((center * center).astype(BF), jnp.ones((C, C), BF)) * (1.0 / C)
    return center * lax.rsqrt(spread + 1e-05)


def gelu(x):
    return 0.5 * x * (1.0 + lax.erf(x * 0.7071067811865476))


def iota(shape, dim):
    return lax.broadcasted_iota(jnp.int32, shape, dim)


def qk(q, k):
    n = q.shape[0]
    parts = []
    for lo, hi in ((0, 128), (128, C)):
        lane = iota((1, hi - lo), 1)
        stack = []
        for h in range((hi - lo) // HEAD_DIM):
            hit = (lane >= h * HEAD_DIM) & (lane < (h + 1) * HEAD_DIM)
            stack.append(q[:, lo:hi] * hit.astype(F32).astype(BF))
        res = mm_nt(jnp.concatenate(stack, axis=0), k[:, lo:hi])
        parts += [res[h * n : (h + 1) * n] for h in range(len(stack))]
    return parts


WIDE = 256


def value_mask(h):
    lane = iota((1, WIDE), 1)
    hit = (lane >= h * HEAD_DIM) & (lane < (h + 1) * HEAD_DIM) | (lane == C + h)
    if h == 0:
        hit = hit | (lane >= C + HEADS)
    return hit.astype(F32).astype(BF)


def divide(acc):
    tail = acc[:, 128:]
    inv = 1.0 / jnp.where(iota((1, 128), 1) >= 64, tail, 1.0)
    high = inv.astype(BF)
    low = (inv - high.astype(F32)).astype(BF)
    i, lane = iota((128, C), 0), iota((128, C), 1)
    first = (i - 64) * HEAD_DIM
    spread = ((lane >= first) & (lane < first + HEAD_DIM)).astype(F32).astype(BF)
    return (acc[:, :C] * (mm(high, spread) + mm(low, spread))).astype(BF)


def tile_bits(shape, dim):
    s = iota(shape, dim)
    return s >> 2, (s >> 1) & 1, s & 1


def build_bias(block, t, sc, tab, out_ref, cut):
    lat, lats = sc[2, 0], sc.shape[1]
    for h in range(HEADS):
        rows = tab[h].astype(F32)
        for p1 in range(2):
            for p2 in range(2):
                for i1 in range(WLAT):
                    a = ((p1 * 2 + p2) * WLAT + i1) * SPAN
                    at = (p1 * WLAT + i1) * 16
                    cut[h, p2, at : at + 16, :] = rows[:, a : a + SPAN].astype(BF)
    n, src = 2 * COL, 2 * WLAT * 16
    o, s = iota((n, src), 0), iota((n, src), 1)
    lw = (o >= COL).astype(jnp.int32)
    q = o - COL * lw
    r1 = 2 * (q >> 3) + ((q >> 2) & 1)
    p1 = (q & 1) ^ block
    own = r1 >= t
    i1 = jnp.where(own, r1 - t, r1 - t + WLAT)
    north = lax.rem(lat + lats - 1, lats)
    kind = jnp.where(
        lw == 0,
        jnp.where(own, sc[0, lat], sc[0, north]),
        jnp.where(own, sc[1, lat], sc[1, north]),
    )
    hit = s == (p1 * WLAT + i1) * 16 + kind
    cell = (q >> 1) & 1
    picks = [(hit & (cell == b)).astype(F32).astype(BF) for b in range(2)]
    pick2 = jnp.concatenate(picks, axis=0)
    left = [[[], []], [[], []]]
    for p2 in range(2):
        for h in range(HEADS):
            both = mm(pick2, cut[h, p2]).astype(BF)
            for b in range(2):
                left[b][p2].append(both[b * n : (b + 1) * n])
    left = [[jnp.concatenate(x, axis=0) for x in y] for y in left]
    m = iota((1, WIN), 1)
    cp2 = (m * 171) >> 12
    u = m - cp2 * COL
    r2 = 2 * (u >> 3) + ((u >> 2) & 1)
    j2 = 2 * cp2 + (((u >> 1) & 1) ^ block)
    p2m = (u & 1) ^ block
    i2 = jnp.where(r2 >= t, r2 - t, r2 - t + WLAT)
    place = i2 * (2 * WLON - 1) + (WLON - 1) - j2
    k = iota((SPAN, WIN), 0)
    mask = None
    if block:
        o = iota((n, WIN), 0)
        lw = (o >= COL).astype(jnp.int32)
        q = o - COL * lw
        r1 = 2 * (q >> 3) + ((q >> 2) & 1)
        south = r1 >= t
        edge = (south & (lat == lats - 1)) | (~south & (lat == 0))
        dead = (lw == 1) & (((q & 1) ^ block) != p2m)
        dead = dead | (edge & ((r1 < t) != (r2 < t)))
        mask = jnp.where(dead, NEG, 0.0).astype(F32)
        mask = jnp.concatenate([mask] * HEADS, axis=0)
    for cp1 in range(PAIRS):
        acc = None
        for b in range(2):
            j1 = 2 * cp1 + (b ^ block)
            for p2 in range(2):
                target = jnp.where(p2m == p2, place + j1, -1)
                pick = (k == target).astype(F32).astype(BF)
                term = mm(left[b][p2], pick)
                acc = term if acc is None else acc + term
        acc = acc * LOG2E
        if block:
            acc = acc + mask
        for h in range(HEADS):
            for lw in range(2):
                out_ref[lw, h, cp1] = acc[(2 * h + lw) * COL : (2 * h + lw + 1) * COL]


VM = pl.BlockSpec(memory_space=pltpu.VMEM)
SM = pl.BlockSpec(memory_space=pltpu.SMEM)


BIAS_SHAPE = (2, HEADS, PAIRS, COL, WIN)
CUT_SHAPE = (HEADS, 2, 2 * WLAT * 16, SPAN)


def ffn(block, mid, up, down, step):
    h_in = norm(mid).astype(BF)
    out = mid
    for f in range(0, FF, step):
        hid = gelu(mm(h_in, up[block, :, f : f + step])).astype(BF)
        out = out + mm_nt(hid, down[block, :, f : f + step])
    return out.astype(BF).astype(F32)


def weights_of(z):
    return jnp.exp2(z - jnp.max(z, axis=-1, keepdims=True)).astype(BF)


def split_point(rows):
    return (rows // 2 + 15) // 16 * 16


def fold(y):
    rows = y.shape[0]
    half = split_point(rows)
    tail = jnp.concatenate([y[half:, 128:], jnp.zeros((2 * half - rows, 64), F32)], axis=0)
    high = jnp.concatenate([y[:half, 128:], tail], axis=1)
    return jnp.concatenate([y[:, :128], high], axis=0).astype(BF)


def unfold(data, rows):
    half = data.shape[0] - rows
    high = jnp.concatenate([data[rows:, :64], data[rows : 2 * rows - half, 64:]], axis=0)
    return jnp.concatenate([data[:rows], high], axis=1)


def tiles_of(ref, rp, k):
    two = jnp.concatenate(
        [ref[2 * rp + d, :, 2 * k * C : 2 * (k + 1) * C].astype(F32) for d in range(2)], axis=0
    )
    a, b = two[:, :C], two[:, C:]
    low = (iota((TILE, 1), 0) & 3) < 2
    return jnp.where(low, a, pltpu.roll(b, 2, 0)), jnp.where(low, pltpu.roll(a, 6, 0), b)


def project(x, w, block, at):
    return mm(x, w[block, :, at * C : (at + 1) * C])


def attend0(wins, step, bias, wqkv, wproj, up, down, x_s, q_s, k_s, v_s, acc_s):
    n = x_s.shape[1] * COL
    v_s[:, C:] = jnp.ones((2 * n, WIDE - C), BF)
    outs = []
    for lw in range(2):
        at = slice(lw * n, (lw + 1) * n)
        xn = norm(x_s[lw].reshape(n, C)).astype(BF)
        q_s[at, :] = (project(xn, wqkv, 0, 0) * (HEAD_DIM**-0.5 * LOG2E)).astype(BF)
        k_s[at, :] = project(xn, wqkv, 0, 1).astype(BF)
        v_s[at, :C] = project(xn, wqkv, 0, 2).astype(BF)
    for lw in range(2):
        done, base = 0, []
        for first, skip in wins:
            at = lw * n + first * COL
            rows = WIN - skip * COL
            q = q_s[at : at + WIN, :]
            if skip:
                q = q.astype(F32)[skip * COL :].astype(BF)
            scores = qk(q, k_s[at : at + WIN, :])
            v = v_s[at : at + WIN, :]
            acc = None
            for h in range(HEADS):
                z = scores[h] + bias[lw, h, skip:].reshape(rows, WIN)
                term = mm(weights_of(z), v * value_mask(h))
                acc = term if acc is None else acc + term
            acc_s[done : done + rows, :] = acc
            done += rows
            base.append(x_s[lw, first + skip : first + PAIRS].reshape(rows, C))
        att = mm(divide(acc_s[:done, :]), wproj[0])
        outs.append(ffn(0, jnp.concatenate(base, axis=0) + att, up, down, step))
    return outs


def own_kernel(
    x, bias, wqkv, wproj, up, down, f_ref, n_ref, x_s, q_s, k_s, v_s, acc_s,
):
    cps = x_s.shape[1]
    for cp in range(cps):
        for rp in range(RPS):
            x_s[0, cp, rp], x_s[1, cp, rp] = tiles_of(x, rp, cp)
    wins = [(i, 0) for i in range(0, cps, PAIRS)]
    outs = attend0(wins, FF, bias, wqkv, wproj, up, down, x_s, q_s, k_s, v_s, acc_s)
    for lw in range(2):
        f_ref[lw] = outs[lw].reshape(cps, RPS, TILE, C)
        n_ref[lw] = norm(outs[lw]).reshape(cps, RPS, TILE, C)


def edge_kernel(
    east, west, bias, n_own, wqkv, wproj, up, down,
    ext_ref, dn_ref, up_ref, x_s, q_s, k_s, v_s, acc_s,
):
    own = n_own.shape[1]
    for cp in range(2 * PAIRS):
        ref, k = (east, cp) if cp < PAIRS else (west, own - 2 * PAIRS + cp)
        for rp in range(RPS):
            x_s[0, cp, rp], x_s[1, cp, rp] = tiles_of(ref, rp, k)
    wins = [(0, 0), (PAIRS, PAIRS - 1)]
    outs = attend0(wins, 256, bias, wqkv, wproj, up, down, x_s, q_s, k_s, v_s, acc_s)
    side = [norm(o).reshape(-1, RPS, TILE, C) for o in outs]
    _, cell, level = tile_bits((1, 1, TILE, 1), 2)
    keep = [level == 1, level == 0]
    for w in range(2):
        pick = lambda a: jnp.where(keep[w], a[0], a[1])
        beside = pick(side)
        o = jnp.concatenate([beside[PAIRS:], pick(n_own), beside[:PAIRS]], axis=0)
        ext_ref[w] = jnp.where(cell == 0, o[1:], o[:-1])
    e = [ext_ref[w] for w in range(2)]
    top = (iota((1, TILE, 1), 1)) < 4
    flat = lambda a: a.reshape(-1, C)
    roll4 = lambda a: pltpu.roll(a, 4, 1)
    half = jnp.where(top, e[0][:, 2], roll4(e[1][:, 2]))
    up_ref[...] = fold(jnp.concatenate([flat(e[0][:, :2]), flat(e[1][:, :2]), flat(half)], axis=0))
    half = jnp.where(top, roll4(e[1][:, 0]), e[0][:, 0])
    dn_ref[...] = fold(jnp.concatenate([flat(e[0][:, 1:]), flat(e[1][:, 1:]), flat(half)], axis=0))


def row_of_tile():
    shape = (1, RPS, TILE, 1)
    return 2 * iota(shape, 1) + tile_bits(shape, 2)[0]


def tiles(a):
    return a.reshape(-1, RPS, TILE, a.shape[-1])


def same_side(t):
    def south(m):
        u = m - ((m * 171) >> 12) * COL
        return (2 * (u >> 3) + ((u >> 2) & 1) >= t).astype(jnp.int32)

    return south(iota((WIN, WIN), 0)) == south(iota((WIN, WIN), 1))


def late_rows():
    return ((iota((COL, 1), 0) >> 1) & 1) == 1


def swap_top(scores, edge):
    top = jnp.where(late_rows(), edge, scores[:COL])
    return jnp.concatenate([top, scores[COL:]], axis=0)


def ready_kernel(sh, sc, tab, ext, f_own, wqkv, z_ref, f_ref, v_ref, q_ref, bias, cut, k_s):
    own = q_ref.shape[0] // 2 // COL
    n = ext.shape[1] * COL
    _, cell, level = tile_bits((1, 1, TILE, 1), 2)
    for w in range(2):
        mine = jnp.where(level == 1 - w, f_own[0], f_own[1])
        before = jnp.concatenate([mine[own - 1 :], mine[: own - 1]], axis=0)
        f_ref[w] = jnp.where(cell == 0, mine, before)
        x = ext[w].reshape(n, C).astype(BF)
        k_s[w * n : (w + 1) * n, :] = project(x, wqkv, 1, 1).astype(BF)
        v_ref[w * n : (w + 1) * n, :] = project(x, wqkv, 1, 2)
        fix = jnp.where(cell == 0, ext[w, :1], ext[w, own : own + 1])
        x = jnp.concatenate([fix, ext[w, 1:own]], axis=0).reshape(-1, C).astype(BF)
        q = project(x, wqkv, 1, 0) * (HEAD_DIM**-0.5 * LOG2E)
        q_ref[w * own * COL : (w + 1) * own * COL, :] = q.astype(BF)
    build_bias(1, sh[0], sc, tab, bias, cut)
    same = same_side(sh[0])
    last = own // PAIRS
    for w in range(2):
        for i in range(last):
            q = q_ref[w * own * COL + i * WIN : w * own * COL + (i + 1) * WIN, :]
            pick = lambda j: k_s[w * n + j * WIN : w * n + (j + 1) * WIN, :]
            scores = qk(q, pick(i))
            if i == 0:
                edge = qk(q.astype(F32)[:COL].astype(BF), pick(last))
                scores = [swap_top(a, b) for a, b in zip(scores, edge)]
            for h in range(HEADS):
                z_ref[w, i, h] = jnp.where(same, scores[h], 0.0) + bias[w, h].reshape(WIN, WIN)


def second_kernel(
    sh, f1, below, above, z_ref, v_own, q_ref, wqkv, wproj, up, down,
    out, k_s, vs_s, vn_s, r_s, acc_s,
):
    t = sh[0]
    own = f1.shape[1]
    n = v_own.shape[0] // 2
    wide = n // COL
    south = unfold(below[...].astype(F32), 2 * wide * 20)
    north = unfold(above[...].astype(F32), 2 * wide * 20)
    full = wide * 16
    roll4 = lambda a: pltpu.roll(a, 4, 1)

    def halves(y):
        rest = y[2 * full :].reshape(wide, TILE, C)
        return [y[w * full : (w + 1) * full].reshape(wide, 2, TILE, C) for w in range(2)], rest

    (s_full, s_half), (n_full, n_half) = halves(south), halves(north)
    lower = row_of_tile() >= t
    cell = tile_bits((1, 1, TILE, 1), 2)[1]
    for w in range(2):
        low = jnp.concatenate(
            [s_full[w], (roll4(s_half) if w else s_half)[:, None]], axis=1)
        high = jnp.concatenate(
            [(roll4(n_half) if w else n_half)[:, None], n_full[w]], axis=1)
        x = jnp.where(lower, high, low).reshape(n, C).astype(BF)
        at = slice(w * n, (w + 1) * n)
        k_s[at, :] = project(x, wqkv, 1, 1).astype(BF)
        mine, other = tiles(v_own[at, :]), tiles(project(x, wqkv, 1, 2))
        vs_s[at, :C] = jnp.where(lower, mine, other).reshape(n, C).astype(BF)
        vn_s[at, :C] = jnp.where(lower, other, mine).reshape(n, C).astype(BF)
    vs_s[:, C:] = vn_s[:, C:] = jnp.ones((2 * n, WIDE - C), BF)
    same = same_side(t)
    last = own // PAIRS
    for w in range(2):
        for i in range(own // PAIRS):
            at = slice(w * own * COL + i * WIN, w * own * COL + (i + 1) * WIN)
            q = q_ref[at, :]
            pick = lambda ref, j: ref[w * n + j * WIN : w * n + (j + 1) * WIN, :]
            scores = qk(q, pick(k_s, i))
            vs, vn = pick(vs_s, i), pick(vn_s, i)
            if i == 0:
                edge = qk(q.astype(F32)[:COL].astype(BF), pick(k_s, last))
                scores = [swap_top(a, b) for a, b in zip(scores, edge)]
                vs2, vn2 = pick(vs_s, last), pick(vn_s, last)
                fix_s, fix_n = jnp.zeros((COL, WIDE), F32), jnp.zeros((COL, WIDE), F32)
            sum_s = sum_n = None
            for h in range(HEADS):
                p = weights_of(z_ref[w, i, h] + jnp.where(same, 0.0, scores[h]))
                hm = value_mask(h)
                ts, tn = mm(p, vs * hm), mm(p, vn * hm)
                sum_s = ts if sum_s is None else sum_s + ts
                sum_n = tn if sum_n is None else sum_n + tn
                if i == 0:
                    p2 = p.astype(F32)[:COL].astype(BF)
                    fix_s = fix_s + mm(p2, vs2 * hm)
                    fix_n = fix_n + mm(p2, vn2 * hm)
            acc = jnp.where(lower, tiles(sum_s), tiles(sum_n))
            if i == 0:
                fix = jnp.where(lower, tiles(fix_s), tiles(fix_n))
                acc = jnp.concatenate([jnp.where(cell == 0, acc[:1], fix), acc[1:]], axis=0)
            acc_s[i * WIN : (i + 1) * WIN, :] = acc.reshape(WIN, WIDE)
        att = mm(divide(acc_s[...]), wproj[1])
        r_s[w] = tiles(ffn(1, f1[w].reshape(-1, C) + att, up, down, FF))
    low = (iota((TILE, 1), 0) & 3) < 2
    _, cell, level = tile_bits((TILE, 1), 0)
    for k in range(own):
        nxt = (k + 1) % own
        for rp in range(RPS):
            n0, n1 = (jnp.where(cell == 0, r_s[w, k, rp], r_s[w, nxt, rp]) for w in range(2))
            t0, t1 = jnp.where(level == 1, n0, n1), jnp.where(level == 0, n0, n1)
            a = jnp.where(low, t0, pltpu.roll(t1, 2, 0))
            b = jnp.where(low, pltpu.roll(t0, 6, 0), t1)
            pair = jnp.concatenate([a, b], axis=1)
            for d in range(2):
                out[2 * rp + d, :, 2 * k * C : 2 * (k + 1) * C] = pair[4 * d : 4 * d + 4].astype(BF)


VM = pl.BlockSpec(memory_space=pltpu.VMEM)
SM = pl.BlockSpec(memory_space=pltpu.SMEM)


def call(kernel, scalars, args, outs, scratch, name, flops):
    return pl.pallas_call(
        kernel,
        out_shape=outs,
        in_specs=[SM] * len(scalars) + [VM] * len(args),
        out_specs=[VM] * len(outs),
        scratch_shapes=scratch,
        compiler_params=pltpu.CompilerParams(vmem_limit_bytes=24 * 2**20),
        cost_estimate=pl.CostEstimate(
            flops=flops, bytes_accessed=4 * 10**6, transcendentals=10**6
        ),
        name=name,
    )(*scalars, *args)


def shifted(x, axis, by):
    size = lax.axis_size(axis)
    return lax.ppermute(x, axis, [(i, (i + by) % size) for i in range(size)])


def body(field, shift, window_type, qkv_weight, proj_weight, up_weight, down_weight, bias_table):
    own = field.shape[2] // C // 2
    wide = own + PAIRS
    x = field.transpose(1, 0, 2)
    weights = (qkv_weight, proj_weight, up_weight, down_weight.transpose(0, 2, 1))
    table = bias_table.transpose(0, 2, 1, 3)
    row = iota((3, window_type.shape[1]), 0)
    scalars = jnp.where(
        row == 2, lax.axis_index("lat"), jnp.pad(window_type, ((0, 1), (0, 0))))
    east = shifted(x, "lon", -1)
    west = shifted(x, "lon", 1)
    sds = jax.ShapeDtypeStruct
    rows = 2 * wide * 20
    pay = (rows + split_point(rows), 128)
    tile = lambda cps: (2, cps, RPS, TILE, C)
    cut = pltpu.VMEM(CUT_SHAPE, BF)

    def scratch(cps, rows):
        n = 2 * cps * COL
        return [pltpu.VMEM(tile(cps), F32), pltpu.VMEM((n, C), BF), pltpu.VMEM((n, C), BF),
                pltpu.VMEM((n, WIDE), BF), pltpu.VMEM((rows, WIDE), F32)]

    (bias0,) = call(
        functools.partial(build_bias, 0, 0), (scalars,), (table[0],), [sds(BIAS_SHAPE, F32)], [cut],
        "bias0", 10**9)
    f_own, n_own = call(
        own_kernel, (), (x, bias0) + weights, [sds(tile(own), F32), sds(tile(own), F32)],
        scratch(own, own * COL), "own0", 2 * 10**9)
    ext, pay_dn, pay_up = call(
        edge_kernel, (), (east, west, bias0, n_own) + weights,
        [sds(tile(wide), F32), sds(pay, BF), sds(pay, BF)],
        scratch(2 * PAIRS, WIN + COL), "edge0", 2 * 10**9)
    above = shifted(pay_dn, "lat", 1)
    below = shifted(pay_up, "lat", -1)
    m, n = 2 * wide * COL, 2 * own * COL
    z_shape = (2, own // PAIRS, HEADS, WIN, WIN)
    z1, f1, v_own, q1 = call(
        ready_kernel, (shift, scalars), (table[1], ext, f_own, qkv_weight),
        [sds(z_shape, F32), sds(tile(own), F32), sds((m, C), F32), sds((n, C), BF)],
        [pltpu.VMEM(BIAS_SHAPE, F32), cut, pltpu.VMEM((m, C), BF)], "ready1", 2 * 10**9)
    (out,) = call(
        second_kernel, (shift,), (f1, below, above, z1, v_own, q1) + weights,
        [sds(x.shape, BF)],
        [pltpu.VMEM((m, lanes), BF) for lanes in (C, WIDE, WIDE)]
        + [pltpu.VMEM(tile(own), F32), pltpu.VMEM((own * COL, WIDE), F32)],
        "block1", 2 * 10**9)
    return out.transpose(1, 0, 2)


def solution(mesh):
    return jax.shard_map(
        body,
        mesh=mesh,
        in_specs=(P(None, "lat", "lon"), P(), P(), P(), P(), P(), P(), P()),
        out_specs=P(None, "lat", "lon"),
        check_vma=False,
    )
```

```python
import functools

import jax
import jax.numpy as jnp
from jax import lax
from jax.experimental import pallas as pl
from jax.experimental.pallas import tpu as pltpu
from jax.sharding import PartitionSpec as P


HEADS = 6
HEAD_DIM = 32
C = 192
FF = 768
WLAT = 6
WLON = 12
TILE = 8
PAIRS = WLON // 2
RPS = WLAT // 2
COL = RPS * TILE
WIN = PAIRS * COL
SPAN = WLAT * (2 * WLON - 1)
NEG = -1e30
LOG2E = 1.4426950408889634
F32 = jnp.float32
BF = jnp.bfloat16


def mm(a, b):
    return jnp.dot(a, b, preferred_element_type=F32)


def mm_nt(a, b):
    return lax.dot_general(a, b, (((1,), (1,)), ((), ())), preferred_element_type=F32)


def norm(x):
    center = x - jnp.mean(x, axis=-1, keepdims=True)
    spread = mm((center * center).astype(BF), jnp.ones((C, C), BF)) * (1.0 / C)
    return center * lax.rsqrt(spread + 1e-05)


def gelu(x):
    return 0.5 * x * (1.0 + lax.erf(x * 0.7071067811865476))


def iota(shape, dim):
    return lax.broadcasted_iota(jnp.int32, shape, dim)


def qk(q, k):
    n = q.shape[0]
    parts = []
    for lo, hi in ((0, 128), (128, C)):
        lane = iota((1, hi - lo), 1)
        stack = []
        for h in range((hi - lo) // HEAD_DIM):
            hit = (lane >= h * HEAD_DIM) & (lane < (h + 1) * HEAD_DIM)
            stack.append(q[:, lo:hi] * hit.astype(F32).astype(BF))
        res = mm_nt(jnp.concatenate(stack, axis=0), k[:, lo:hi])
        parts += [res[h * n : (h + 1) * n] for h in range(len(stack))]
    return parts


WIDE = 256


def value_mask(h):
    lane = iota((1, WIDE), 1)
    hit = (lane >= h * HEAD_DIM) & (lane < (h + 1) * HEAD_DIM) | (lane == C + h)
    if h == 0:
        hit = hit | (lane >= C + HEADS)
    return hit.astype(F32).astype(BF)


def divide(acc):
    tail = acc[:, 128:]
    inv = 1.0 / jnp.where(iota((1, 128), 1) >= 64, tail, 1.0)
    high = inv.astype(BF)
    low = (inv - high.astype(F32)).astype(BF)
    i, lane = iota((128, C), 0), iota((128, C), 1)
    first = (i - 64) * HEAD_DIM
    spread = ((lane >= first) & (lane < first + HEAD_DIM)).astype(F32).astype(BF)
    return (acc[:, :C] * (mm(high, spread) + mm(low, spread))).astype(BF)


def tile_bits(shape, dim):
    s = iota(shape, dim)
    return s >> 2, (s >> 1) & 1, s & 1


def build_bias(block, t, sc, tab, out_ref, cut):
    lat, lats = sc[2, 0], sc.shape[1]
    for h in range(HEADS):
        rows = tab[h].astype(F32)
        for p1 in range(2):
            for p2 in range(2):
                for i1 in range(WLAT):
                    a = ((p1 * 2 + p2) * WLAT + i1) * SPAN
                    at = (p1 * WLAT + i1) * 16
                    cut[h, p2, at : at + 16, :] = rows[:, a : a + SPAN].astype(BF)
    n, src = 2 * COL, 2 * WLAT * 16
    o, s = iota((n, src), 0), iota((n, src), 1)
    lw = (o >= COL).astype(jnp.int32)
    q = o - COL * lw
    r1 = 2 * (q >> 3) + ((q >> 2) & 1)
    p1 = (q & 1) ^ block
    own = r1 >= t
    i1 = jnp.where(own, r1 - t, r1 - t + WLAT)
    north = lax.rem(lat + lats - 1, lats)
    kind = jnp.where(
        lw == 0,
        jnp.where(own, sc[0, lat], sc[0, north]),
        jnp.where(own, sc[1, lat], sc[1, north]),
    )
    hit = s == (p1 * WLAT + i1) * 16 + kind
    cell = (q >> 1) & 1
    picks = [(hit & (cell == b)).astype(F32).astype(BF) for b in range(2)]
    pick2 = jnp.concatenate(picks, axis=0)
    left = [[[], []], [[], []]]
    for p2 in range(2):
        for h in range(HEADS):
            both = mm(pick2, cut[h, p2]).astype(BF)
            for b in range(2):
                left[b][p2].append(both[b * n : (b + 1) * n])
    left = [[jnp.concatenate(x, axis=0) for x in y] for y in left]
    m = iota((1, WIN), 1)
    cp2 = (m * 171) >> 12
    u = m - cp2 * COL
    r2 = 2 * (u >> 3) + ((u >> 2) & 1)
    j2 = 2 * cp2 + (((u >> 1) & 1) ^ block)
    p2m = (u & 1) ^ block
    i2 = jnp.where(r2 >= t, r2 - t, r2 - t + WLAT)
    place = i2 * (2 * WLON - 1) + (WLON - 1) - j2
    k = iota((SPAN, WIN), 0)
    mask = None
    if block:
        o = iota((n, WIN), 0)
        lw = (o >= COL).astype(jnp.int32)
        q = o - COL * lw
        r1 = 2 * (q >> 3) + ((q >> 2) & 1)
        south = r1 >= t
        edge = (south & (lat == lats - 1)) | (~south & (lat == 0))
        dead = (lw == 1) & (((q & 1) ^ block) != p2m)
        dead = dead | (edge & ((r1 < t) != (r2 < t)))
        mask = jnp.where(dead, NEG, 0.0).astype(F32)
        mask = jnp.concatenate([mask] * HEADS, axis=0)
    for cp1 in range(PAIRS):
        acc = None
        for b in range(2):
            j1 = 2 * cp1 + (b ^ block)
            for p2 in range(2):
                target = jnp.where(p2m == p2, place + j1, -1)
                pick = (k == target).astype(F32).astype(BF)
                term = mm(left[b][p2], pick)
                acc = term if acc is None else acc + term
        acc = acc * LOG2E
        if block:
            acc = acc + mask
        for h in range(HEADS):
            for lw in range(2):
                out_ref[lw, h, cp1] = acc[(2 * h + lw) * COL : (2 * h + lw + 1) * COL]


VM = pl.BlockSpec(memory_space=pltpu.VMEM)
SM = pl.BlockSpec(memory_space=pltpu.SMEM)


BIAS_SHAPE = (2, HEADS, PAIRS, COL, WIN)
CUT_SHAPE = (HEADS, 2, 2 * WLAT * 16, SPAN)


def ffn(block, mid, up, down, step):
    h_in = norm(mid).astype(BF)
    out = mid
    for f in range(0, FF, step):
        hid = gelu(mm(h_in, up[block, :, f : f + step])).astype(BF)
        out = out + mm_nt(hid, down[block, :, f : f + step])
    return out.astype(BF).astype(F32)


def weights_of(z):
    return jnp.exp2(z - jnp.max(z, axis=-1, keepdims=True)).astype(BF)


def split_point(rows):
    return (rows // 2 + 15) // 16 * 16


def fold(y):
    rows = y.shape[0]
    half = split_point(rows)
    tail = jnp.concatenate([y[half:, 128:], jnp.zeros((2 * half - rows, 64), F32)], axis=0)
    high = jnp.concatenate([y[:half, 128:], tail], axis=1)
    return jnp.concatenate([y[:, :128], high], axis=0).astype(BF)


def unfold(data, rows):
    half = data.shape[0] - rows
    high = jnp.concatenate([data[rows:, :64], data[rows : 2 * rows - half, 64:]], axis=0)
    return jnp.concatenate([data[:rows], high], axis=1)


def tiles_of(ref, rp, k):
    two = jnp.concatenate(
        [ref[2 * rp + d, :, 2 * k * C : 2 * (k + 1) * C].astype(F32) for d in range(2)], axis=0
    )
    a, b = two[:, :C], two[:, C:]
    low = (iota((TILE, 1), 0) & 3) < 2
    return jnp.where(low, a, pltpu.roll(b, 2, 0)), jnp.where(low, pltpu.roll(a, 6, 0), b)


def project(x, w, block, at):
    return mm(x, w[block, :, at * C : (at + 1) * C])


def attend0(wins, step, bias, wqkv, wproj, up, down, x_s, q_s, k_s, v_s, acc_s):
    n = x_s.shape[1] * COL
    v_s[:, C:] = jnp.ones((2 * n, WIDE - C), BF)
    outs = []
    for lw in range(2):
        at = slice(lw * n, (lw + 1) * n)
        xn = norm(x_s[lw].reshape(n, C)).astype(BF)
        q_s[at, :] = (project(xn, wqkv, 0, 0) * (HEAD_DIM**-0.5 * LOG2E)).astype(BF)
        k_s[at, :] = project(xn, wqkv, 0, 1).astype(BF)
        v_s[at, :C] = project(xn, wqkv, 0, 2).astype(BF)
    for lw in range(2):
        done, base = 0, []
        for first, skip in wins:
            at = lw * n + first * COL
            rows = WIN - skip * COL
            q = q_s[at : at + WIN, :]
            if skip:
                q = q.astype(F32)[skip * COL :].astype(BF)
            scores = qk(q, k_s[at : at + WIN, :])
            v = v_s[at : at + WIN, :]
            acc = None
            for h in range(HEADS):
                z = scores[h] + bias[lw, h, skip:].reshape(rows, WIN)
                term = mm(weights_of(z), v * value_mask(h))
                acc = term if acc is None else acc + term
            acc_s[done : done + rows, :] = acc
            done += rows
            base.append(x_s[lw, first + skip : first + PAIRS].reshape(rows, C))
        att = mm(divide(acc_s[:done, :]), wproj[0])
        outs.append(ffn(0, jnp.concatenate(base, axis=0) + att, up, down, step))
    return outs


def own_kernel(
    x, bias, wqkv, wproj, up, down, f_ref, n_ref, x_s, q_s, k_s, v_s, acc_s,
):
    cps = x_s.shape[1]
    for cp in range(cps):
        for rp in range(RPS):
            x_s[0, cp, rp], x_s[1, cp, rp] = tiles_of(x, rp, cp)
    wins = [(i, 0) for i in range(0, cps, PAIRS)]
    outs = attend0(wins, FF, bias, wqkv, wproj, up, down, x_s, q_s, k_s, v_s, acc_s)
    for lw in range(2):
        f_ref[lw] = outs[lw].reshape(cps, RPS, TILE, C)
        n_ref[lw] = norm(outs[lw]).reshape(cps, RPS, TILE, C)


def edge_kernel(
    west, east, bias, n_own, wqkv, wproj, up, down,
    ext_ref, up_ref, dn_ref, x_s, q_s, k_s, v_s, acc_s,
):
    own = n_own.shape[1]
    for cp in range(2 * PAIRS):
        ref, k = (east, cp) if cp < PAIRS else (west, own - 2 * PAIRS + cp)
        for rp in range(RPS):
            x_s[0, cp, rp], x_s[1, cp, rp] = tiles_of(ref, rp, k)
    wins = [(0, 0), (PAIRS, PAIRS - 1)]
    outs = attend0(wins, 256, bias, wqkv, wproj, up, down, x_s, q_s, k_s, v_s, acc_s)
    side = [norm(o).reshape(-1, RPS, TILE, C) for o in outs]
    _, cell, level = tile_bits((1, 1, TILE, 1), 2)
    keep = [level == 1, level == 0]
    for w in range(2):
        pick = lambda a: jnp.where(keep[w], a[0], a[1])
        beside = pick(side)
        o = jnp.concatenate([beside[PAIRS:], pick(n_own), beside[:PAIRS]], axis=0)
        ext_ref[w] = jnp.where(cell == 0, o[1:], o[:-1])
    e = [ext_ref[w] for w in range(2)]
    top = (iota((1, TILE, 1), 1)) < 4
    flat = lambda a: a.reshape(-1, C)
    roll4 = lambda a: pltpu.roll(a, 4, 1)
    half = jnp.where(top, e[0][:, 2], roll4(e[1][:, 2]))
    up_ref[...] = fold(jnp.concatenate([flat(e[0][:, :2]), flat(e[1][:, :2]), flat(half)], axis=0))
    half = jnp.where(top, roll4(e[1][:, 0]), e[0][:, 0])
    dn_ref[...] = fold(jnp.concatenate([flat(e[0][:, 1:]), flat(e[1][:, 1:]), flat(half)], axis=0))


def row_of_tile():
    shape = (1, RPS, TILE, 1)
    return 2 * iota(shape, 1) + tile_bits(shape, 2)[0]


def tiles(a):
    return a.reshape(-1, RPS, TILE, a.shape[-1])


def same_side(t):
    def south(m):
        u = m - ((m * 171) >> 12) * COL
        return (2 * (u >> 3) + ((u >> 2) & 1) >= t).astype(jnp.int32)

    return south(iota((WIN, WIN), 0)) == south(iota((WIN, WIN), 1))


def late_rows():
    return ((iota((COL, 1), 0) >> 1) & 1) == 1


def swap_top(scores, edge):
    top = jnp.where(late_rows(), edge, scores[:COL])
    return jnp.concatenate([top, scores[COL:]], axis=0)


def ready_kernel(sh, sc, tab, ext, f_own, wqkv, z_ref, f_ref, v_ref, q_ref, bias, cut, k_s):
    own = q_ref.shape[0] // 2 // COL
    n = ext.shape[1] * COL
    _, cell, level = tile_bits((1, 1, TILE, 1), 2)
    for w in range(2):
        mine = jnp.where(level == 1 - w, f_own[0], f_own[1])
        before = jnp.concatenate([mine[own - 1 :], mine[: own - 1]], axis=0)
        f_ref[w] = jnp.where(cell == 0, mine, before)
        x = ext[w].reshape(n, C).astype(BF)
        k_s[w * n : (w + 1) * n, :] = project(x, wqkv, 1, 1).astype(BF)
        v_ref[w * n : (w + 1) * n, :] = project(x, wqkv, 1, 2)
        fix = jnp.where(cell == 0, ext[w, :1], ext[w, own : own + 1])
        x = jnp.concatenate([fix, ext[w, 1:own]], axis=0).reshape(-1, C).astype(BF)
        q = project(x, wqkv, 1, 0) * (HEAD_DIM**-0.5 * LOG2E)
        q_ref[w * own * COL : (w + 1) * own * COL, :] = q.astype(BF)
    build_bias(1, sh[0], sc, tab, bias, cut)
    same = same_side(sh[0])
    last = own // PAIRS
    for w in range(2):
        for i in range(last):
            q = q_ref[w * own * COL + i * WIN : w * own * COL + (i + 1) * WIN, :]
            pick = lambda j: k_s[w * n + j * WIN : w * n + (j + 1) * WIN, :]
            scores = qk(q, pick(i))
            if i == 0:
                edge = qk(q.astype(F32)[:COL].astype(BF), pick(last))
                scores = [swap_top(a, b) for a, b in zip(scores, edge)]
            for h in range(HEADS):
                z_ref[w, i, h] = jnp.where(same, scores[h], 0.0) + bias[w, h].reshape(WIN, WIN)


def second_kernel(
    sh, f1, above, below, z_ref, v_own, q_ref, wqkv, wproj, up, down,
    out, k_s, vs_s, vn_s, r_s, acc_s,
):
    t = sh[0]
    own = f1.shape[1]
    n = v_own.shape[0] // 2
    wide = n // COL
    south = unfold(below[...].astype(F32), 2 * wide * 20)
    north = unfold(above[...].astype(F32), 2 * wide * 20)
    full = wide * 16
    roll4 = lambda a: pltpu.roll(a, 4, 1)

    def halves(y):
        rest = y[2 * full :].reshape(wide, TILE, C)
        return [y[w * full : (w + 1) * full].reshape(wide, 2, TILE, C) for w in range(2)], rest

    (s_full, s_half), (n_full, n_half) = halves(south), halves(north)
    lower = row_of_tile() >= t
    cell = tile_bits((1, 1, TILE, 1), 2)[1]
    for w in range(2):
        low = jnp.concatenate(
            [s_full[w], (roll4(s_half) if w else s_half)[:, None]], axis=1)
        high = jnp.concatenate(
            [(roll4(n_half) if w else n_half)[:, None], n_full[w]], axis=1)
        x = jnp.where(lower, high, low).reshape(n, C).astype(BF)
        at = slice(w * n, (w + 1) * n)
        k_s[at, :] = project(x, wqkv, 1, 1).astype(BF)
        mine, other = tiles(v_own[at, :]), tiles(project(x, wqkv, 1, 2))
        vs_s[at, :C] = jnp.where(lower, mine, other).reshape(n, C).astype(BF)
        vn_s[at, :C] = jnp.where(lower, other, mine).reshape(n, C).astype(BF)
    vs_s[:, C:] = vn_s[:, C:] = jnp.ones((2 * n, WIDE - C), BF)
    same = same_side(t)
    last = own // PAIRS
    for w in range(2):
        for i in range(own // PAIRS):
            at = slice(w * own * COL + i * WIN, w * own * COL + (i + 1) * WIN)
            q = q_ref[at, :]
            pick = lambda ref, j: ref[w * n + j * WIN : w * n + (j + 1) * WIN, :]
            scores = qk(q, pick(k_s, i))
            vs, vn = pick(vs_s, i), pick(vn_s, i)
            if i == 0:
                edge = qk(q.astype(F32)[:COL].astype(BF), pick(k_s, last))
                scores = [swap_top(a, b) for a, b in zip(scores, edge)]
                vs2, vn2 = pick(vs_s, last), pick(vn_s, last)
                fix_s, fix_n = jnp.zeros((COL, WIDE), F32), jnp.zeros((COL, WIDE), F32)
            sum_s = sum_n = None
            for h in range(HEADS):
                p = weights_of(z_ref[w, i, h] + jnp.where(same, 0.0, scores[h]))
                hm = value_mask(h)
                ts, tn = mm(p, vs * hm), mm(p, vn * hm)
                sum_s = ts if sum_s is None else sum_s + ts
                sum_n = tn if sum_n is None else sum_n + tn
                if i == 0:
                    p2 = p.astype(F32)[:COL].astype(BF)
                    fix_s = fix_s + mm(p2, vs2 * hm)
                    fix_n = fix_n + mm(p2, vn2 * hm)
            acc = jnp.where(lower, tiles(sum_s), tiles(sum_n))
            if i == 0:
                fix = jnp.where(lower, tiles(fix_s), tiles(fix_n))
                acc = jnp.concatenate([jnp.where(cell == 0, acc[:1], fix), acc[1:]], axis=0)
            acc_s[i * WIN : (i + 1) * WIN, :] = acc.reshape(WIN, WIDE)
        att = mm(divide(acc_s[...]), wproj[1])
        r_s[w] = tiles(ffn(1, f1[w].reshape(-1, C) + att, up, down, FF))
    low = (iota((TILE, 1), 0) & 3) < 2
    _, cell, level = tile_bits((TILE, 1), 0)
    for k in range(own):
        nxt = (k + 1) % own
        for rp in range(RPS):
            n0, n1 = (jnp.where(cell == 0, r_s[w, k, rp], r_s[w, nxt, rp]) for w in range(2))
            t0, t1 = jnp.where(level == 1, n0, n1), jnp.where(level == 0, n0, n1)
            a = jnp.where(low, t0, pltpu.roll(t1, 2, 0))
            b = jnp.where(low, pltpu.roll(t0, 6, 0), t1)
            pair = jnp.concatenate([a, b], axis=1)
            for d in range(2):
                out[2 * rp + d, :, 2 * k * C : 2 * (k + 1) * C] = pair[4 * d : 4 * d + 4].astype(BF)


VM = pl.BlockSpec(memory_space=pltpu.VMEM)
SM = pl.BlockSpec(memory_space=pltpu.SMEM)


def call(kernel, scalars, args, outs, scratch, name, flops):
    return pl.pallas_call(
        kernel,
        out_shape=outs,
        in_specs=[SM] * len(scalars) + [VM] * len(args),
        out_specs=[VM] * len(outs),
        scratch_shapes=scratch,
        compiler_params=pltpu.CompilerParams(vmem_limit_bytes=24 * 2**20),
        cost_estimate=pl.CostEstimate(
            flops=flops, bytes_accessed=4 * 10**6, transcendentals=10**6
        ),
        name=name,
    )(*scalars, *args)


def shifted(x, axis, by):
    size = lax.axis_size(axis)
    return lax.ppermute(x, axis, [(i, (i + by) % size) for i in range(size)])


def body(field, shift, window_type, qkv_weight, proj_weight, up_weight, down_weight, bias_table):
    own = field.shape[2] // C // 2
    wide = own + PAIRS
    x = field.transpose(1, 0, 2)
    weights = (qkv_weight, proj_weight, up_weight, down_weight.transpose(0, 2, 1))
    table = bias_table.transpose(0, 2, 1, 3)
    row = iota((3, window_type.shape[1]), 0)
    scalars = jnp.where(
        row == 2, lax.axis_index("lat"), jnp.pad(window_type, ((0, 1), (0, 0))))
    west = shifted(x, "lon", 1)
    east = shifted(x, "lon", -1)
    sds = jax.ShapeDtypeStruct
    rows = 2 * wide * 20
    pay = (rows + split_point(rows), 128)
    tile = lambda cps: (2, cps, RPS, TILE, C)
    cut = pltpu.VMEM(CUT_SHAPE, BF)

    def scratch(cps, rows):
        n = 2 * cps * COL
        return [pltpu.VMEM(tile(cps), F32), pltpu.VMEM((n, C), BF), pltpu.VMEM((n, C), BF),
                pltpu.VMEM((n, WIDE), BF), pltpu.VMEM((rows, WIDE), F32)]

    (bias0,) = call(
        functools.partial(build_bias, 0, 0), (scalars,), (table[0],), [sds(BIAS_SHAPE, F32)], [cut],
        "bias0", 10**9)
    f_own, n_own = call(
        own_kernel, (), (x, bias0) + weights, [sds(tile(own), F32), sds(tile(own), F32)],
        scratch(own, own * COL), "own0", 2 * 10**9)
    ext, pay_up, pay_dn = call(
        edge_kernel, (), (west, east, bias0, n_own) + weights,
        [sds(tile(wide), F32), sds(pay, BF), sds(pay, BF)],
        scratch(2 * PAIRS, WIN + COL), "edge0", 2 * 10**9)
    below = shifted(pay_up, "lat", -1)
    above = shifted(pay_dn, "lat", 1)
    m, n = 2 * wide * COL, 2 * own * COL
    z_shape = (2, own // PAIRS, HEADS, WIN, WIN)
    z1, f1, v_own, q1 = call(
        ready_kernel, (shift, scalars), (table[1], ext, f_own, qkv_weight),
        [sds(z_shape, F32), sds(tile(own), F32), sds((m, C), F32), sds((n, C), BF)],
        [pltpu.VMEM(BIAS_SHAPE, F32), cut, pltpu.VMEM((m, C), BF)], "ready1", 2 * 10**9)
    (out,) = call(
        second_kernel, (shift,), (f1, above, below, z1, v_own, q1) + weights,
        [sds(x.shape, BF)],
        [pltpu.VMEM((m, lanes), BF) for lanes in (C, WIDE, WIDE)]
        + [pltpu.VMEM(tile(own), F32), pltpu.VMEM((own * COL, WIDE), F32)],
        "block1", 2 * 10**9)
    return out.transpose(1, 0, 2)


def solution(mesh):
    return jax.shard_map(
        body,
        mesh=mesh,
        in_specs=(P(None, "lat", "lon"), P(), P(), P(), P(), P(), P(), P()),
        out_specs=P(None, "lat", "lon"),
        check_vma=False,
    )
```
